768 devices in a mesh: grp: 96 (over z, y), dev: 8 (over x, core).
Axes of the slice: x: 4, y: 8, z: 12, core: 2. Of those that a mesh axis runs over, the one named last changes fastest.
Arguments:
- source: float32 [64, 1536, 128], P('dev', 'grp'), may hold values from -8 to 8
- absorb: float32 [64, 1536, 128], P('dev', 'grp'), may hold values from 0.05 to 0.5
- conduct: float32 [64, 1536, 128], P('dev', 'grp'), may hold values from 0.3 to 3
Outputs:
- fine_solution: float32 [64, 1536, 128], P('dev', 'grp')
- fine_residual: float32 [64, 1536, 128], P('dev', 'grp')
The draws below stay inside these ranges and needn't reach their ends.
All inputs are finite; a program needn't handle non-finite values.
Results may differ from the reference program's by a relative error of at most 0.0003.
Values sent between devices are 32-bit elements; how exact they have to be, the bound alone decides.
No kernel may reach another device: no remote copies, remote signals or barrier semaphores. Data moves between devices by JAX's collectives and lax.ppermute only.
A program may use at most 64 MiB of HBM per device.

```python
import math
import jax
import jax.numpy as jnp

CYCLES = 2
BOTTOM = 4
NX = 64
NY = 1536
NZ = 128


def draw_source(key, part):
    key = jax.random.fold_in(key, 7)
    values = jax.random.normal(key, (NX, NY, NZ), jnp.float32)
    return jnp.clip(values, -8.0, 8.0)


def block_scale(stream_key, dims, cuts, smallest, high):
    def one(dim, blocks):
        heights = jax.random.uniform(jax.random.fold_in(jax.random.fold_in(stream_key, 6), dim), (blocks,), jnp.float32, smallest / len(cuts), high / len(cuts))
        return jnp.repeat(jnp.exp(heights), dims[dim] // blocks).reshape((-1,) + (1,) * (len(dims) - dim - 1))

    factor_of = one(*cuts[0])
    for cut in cuts[1:]:
        factor_of = factor_of * one(*cut)
    return factor_of


def setup_inputs(seed: int = 0) -> dict:
    keys = jax.random.split(jax.random.key(seed), 4)
    return {
        "source": draw_source(jax.random.fold_in(keys[3], 71), 0),
        "absorb": jnp.clip(jnp.exp(math.log(0.5) - 2.3025851 * jax.random.uniform(keys[1], (NX, NY, NZ), jnp.float32) ** block_scale(keys[1], (NX, NY, NZ), ((0, 8), (1, 96)), -0.2, 0.2)), 0.05, 0.5),
        "conduct": jnp.clip(jnp.exp(math.log(3.0) - 2.3025851 * jax.random.uniform(keys[2], (NX, NY, NZ), jnp.float32) ** block_scale(keys[2], (NX, NY, NZ), ((0, 8), (1, 96)), -0.2, 0.2)), 0.3, 3.0),
    }


RELAX = 0.8

NEIGHBOURS = (
    (slice(2, None), slice(1, -1), slice(1, -1)),
    (slice(None, -2), slice(1, -1), slice(1, -1)),
    (slice(1, -1), slice(2, None), slice(1, -1)),
    (slice(1, -1), slice(None, -2), slice(1, -1)),
    (slice(1, -1), slice(1, -1), slice(2, None)),
    (slice(1, -1), slice(1, -1), slice(None, -2)),
)


def pad_plane(field):
    return jnp.pad(field, ((1, 1), (1, 1), (0, 0)))


def stencil_parts(padded_field, padded_coef):
    padded_field = jnp.pad(padded_field, ((0, 0), (0, 0), (1, 1)))
    padded_coef = jnp.pad(padded_coef, ((0, 0), (0, 0), (1, 1)))
    center_field = padded_field[1:-1, 1:-1, 1:-1]
    center_coef = padded_coef[1:-1, 1:-1, 1:-1]
    face_sum = jnp.zeros_like(center_field)
    beside = jnp.zeros_like(center_field)
    for window in NEIGHBOURS:
        face = (center_coef + padded_coef[window]) * 0.5
        face_sum = face_sum + face
        beside = beside + face * padded_field[window]
    return center_field, face_sum, beside


def relax_once(padded_field, padded_coef, absorb, rhs, spacing):
    center_field, face_sum, beside = stencil_parts(padded_field, padded_coef)
    diagonal = absorb + face_sum / spacing
    applied = diagonal * center_field - beside / spacing
    return center_field + RELAX * (rhs - applied) / diagonal


def residual_of(padded_field, padded_coef, absorb, rhs, spacing):
    center_field, face_sum, beside = stencil_parts(padded_field, padded_coef)
    diagonal = absorb + face_sum / spacing
    applied = diagonal * center_field - beside / spacing
    return rhs - applied


def restrict(field):
    size_x, size_y, size_z = field.shape
    blocks = field.reshape(size_x // 2, 2, size_y // 2, 2, size_z // 2, 2)
    return blocks.sum(axis=(1, 3, 5)) * 0.125


def prolong(field):
    return jnp.repeat(jnp.repeat(jnp.repeat(field, 2, 0), 2, 1), 2, 2)


def reference(source, absorb, conduct):
    absorb_mid = restrict(absorb)
    absorb_low = restrict(absorb_mid)
    conduct_mid = restrict(conduct)
    conduct_low = restrict(conduct_mid)
    coef_fine = pad_plane(conduct)
    coef_mid = pad_plane(conduct_mid)
    coef_low = pad_plane(conduct_low)
    fine = jnp.zeros_like(source)
    for turn in range(CYCLES):
        for sweep_index in range(2):
            fine = relax_once(pad_plane(fine), coef_fine, absorb, source, 1.0)
        middle_rhs = restrict(residual_of(pad_plane(fine), coef_fine, absorb, source, 1.0))
        middle = jnp.zeros_like(middle_rhs)
        for sweep_index in range(2):
            middle = relax_once(pad_plane(middle), coef_mid, absorb_mid, middle_rhs, 4.0)
        lowest_rhs = restrict(residual_of(pad_plane(middle), coef_mid, absorb_mid, middle_rhs, 4.0))
        lowest = jnp.zeros_like(lowest_rhs)
        for sweep_index in range(BOTTOM):
            lowest = relax_once(pad_plane(lowest), coef_low, absorb_low, lowest_rhs, 16.0)
        middle = middle + prolong(lowest)
        for sweep_index in range(2):
            middle = relax_once(pad_plane(middle), coef_mid, absorb_mid, middle_rhs, 4.0)
        fine = fine + prolong(middle)
        for sweep_index in range(2):
            fine = relax_once(pad_plane(fine), coef_fine, absorb, source, 1.0)
    final_residual = residual_of(pad_plane(fine), coef_fine, absorb, source, 1.0)
    return fine, final_residual
```

```python
import functools

import jax
import jax.numpy as jnp
from jax import lax
from jax.experimental import pallas as pl
from jax.experimental.pallas import tpu as pltpu
from jax.sharding import PartitionSpec as P

RELAX = 0.8
HALO = 9
ROWS = 16 + 2 * HALO
FX = 24
MROWS = 40
MX = 32
LROWS = 20
LX = 16
VMEM_LIMIT = 40 * 1024 * 1024

F32 = jnp.float32


def rows(lo, hi, body, step=2):
    count = (hi - lo) // step

    def several(i, carry):
        for t in range(step):
            body(lo + i * step + t)
        return carry

    if count > 0:
        lax.fori_loop(0, count, several, 0)
    for y in range(lo + count * step, hi):
        body(y)


def lanes(shape):
    return lax.broadcasted_iota(jnp.int32, shape, 1)


def planes(shape):
    return lax.broadcasted_iota(jnp.int32, shape, 0)


def up(value, axis, by):
    return pltpu.roll(value, value.shape[axis] - by, axis)


def down(value, axis, by):
    return pltpu.roll(value, by, axis)


class Level:
    def __init__(self, bx, by, bz, diag, inv, width):
        self.bx, self.by, self.bz, self.diag, self.inv, self.width = bx, by, bz, diag, inv, width

    def beside(self, u_ref, y):
        u = u_ref[y]
        bx = self.bx[y]
        bz = self.bz[y]
        acc = self.by[y] * u_ref[y + 1] + self.by[y - 1] * u_ref[y - 1]
        acc = acc + (bx * up(u, 0, 1) + down(bx * u, 0, 1))
        acc = acc + (bz * up(u, 1, self.width) + down(bz * u, 1, self.width))
        return u, acc

    def sweep(self, dst, src, rhs, lo, hi):
        def body(y):
            u, acc = self.beside(src, y)
            dst[y] = (1.0 - RELAX) * u + self.inv[y] * (rhs[y] + acc)

        rows(lo, hi, body)

    def residual(self, u_ref, rhs, y):
        u, acc = self.beside(u_ref, y)
        return rhs[y] - self.diag[y] * u + acc

    def build(self, conduct, absorb, lo, hi, spacing, closed, edges=None):
        shape = conduct.shape[1:]
        z, x = lanes(shape), planes(shape)
        half = 0.5 / spacing

        def body(y):
            c = conduct[y]
            xp, xm = up(c, 0, 1), down(c, 0, 1)
            if closed:
                xp = jnp.where(x == shape[0] - 1, 0.0, xp)
                xm = jnp.where(x == 0, 0.0, xm)
            else:
                left, right = edges
                xp = jnp.where(x == shape[0] - 1, right[y], xp)
                xm = jnp.where(x == 0, left[y], xm)
            zp = jnp.where(z >= shape[1] - self.width, 0.0, up(c, 1, self.width))
            zm = jnp.where(z < self.width, 0.0, down(c, 1, self.width))
            yp, ym = conduct[y + 1], conduct[y - 1]
            bx = (c + xp) * half
            self.bx[y] = jnp.where(x == shape[0] - 1, 0.0, bx) if closed else bx
            self.by[y] = (c + yp) * half
            self.bz[y] = jnp.where(z >= shape[1] - self.width, 0.0, (c + zp) * half)
            a = absorb[y]
            diag = a + (3.0 / spacing) * c + half * (((xp + xm) + (yp + ym)) + (zp + zm))
            if self.diag is not None:
                self.diag[y] = diag
            self.inv[y] = jnp.where(a > 0.0, RELAX / diag, 0.0)

        self.by[lo - 1] = (conduct[lo - 1] + conduct[lo]) * half
        rows(lo, hi, body)


def pair_lanes(t, width):
    first = (lanes(t.shape) // width) % 2 == 0
    return t + jnp.where(first, up(t, 1, width), down(t, 1, width))


def pair_planes(t):
    first = planes(t.shape) % 2 == 0
    return t + jnp.where(first, up(t, 0, 1), down(t, 0, 1))


def pack_rows(row_of):
    x, z = planes((8, 128)) % 2, lanes((8, 128)) % 2
    tiles = []
    for k in range(2):
        r = [row_of(4 * k + t) for t in range(4)]
        tiles.append(jnp.where(x == 0, jnp.where(z == 0, r[0], r[1]), jnp.where(z == 0, r[2], r[3])))
    return tiles


def restrict_own(fine_row):
    def row_of(j):
        t = fine_row(2 * j) + fine_row(2 * j + 1)
        return pair_planes(pair_lanes(t, 1)) * 0.125

    return pack_rows(row_of)


def restrict_low(fine_row, tmp, dst, lo, hi):
    def body(i):
        t = pair_lanes(fine_row(2 * i) + fine_row(2 * i + 1), 2)
        tmp[...] = t
        dst[i] = (tmp[pl.ds(0, LX, stride=2), :] + tmp[pl.ds(1, LX, stride=2), :]) * 0.125

    rows(lo, hi, body, 1)


def fine_kernel(scal, own, via_a, via_b, edge_l, edge_r,
                src, bx, by, bz, diag, inv, u2, pack,
                absorb, conduct, u1):
    even = scal[0] == 0

    def join(y):
        for arr, dst in ((0, src), (1, absorb), (2, conduct)):
            a, b = via_a[arr, y], via_b[arr, y]
            dst[y, 0:8, :] = jnp.where(even, b, a)
            dst[y, 8:16, :] = own[arr, y]
            dst[y, 16:24, :] = jnp.where(even, a, b)

    rows(0, ROWS, join)
    level = Level(bx, by, bz, diag, inv, 1)

    class Row:
        def __init__(self, ref):
            self.ref = ref

        def __getitem__(self, y):
            return self.ref[pl.ds(y, 1), :]

    level.build(conduct, absorb, 1, ROWS - 1, 1.0, False, (Row(edge_l), Row(edge_r)))

    def first(y):
        u1[y] = inv[y] * src[y]

    rows(1, ROWS - 1, first)
    zero = jnp.zeros((FX, 128), F32)
    for y in (0, 1, ROWS - 2, ROWS - 1):
        u2[y] = zero
    level.sweep(u2, u1, src, 2, ROWS - 2)
    tiles = restrict_own(lambda i: level.residual(u2, src, HALO + i)[8:16])
    tiles += restrict_own(lambda i: absorb[HALO + i, 8:16, :])
    tiles += restrict_own(lambda i: conduct[HALO + i, 8:16, :])
    for i, t in enumerate(tiles):
        pack[i] = t


def gather_rows(scal, mine, theirs, joined, arrays):
    pos, here, peers = scal[1], scal[2], scal[3]
    zero = jnp.zeros((8, 128), F32)
    for j in range(5):
        at = pos + (j - 2)
        there = here + (j - 2)
        inside = jnp.logical_and(there >= 0, there < peers)
        is_mine = jnp.logical_and(at >= 0, at < 4)

        def copy(source, start):
            for chip in range(4):
                for core in range(2):
                    for t in range(2 * arrays):
                        dev = 2 * chip + core
                        joined[j, t, 8 * dev:8 * dev + 8, :] = source[start * 4 + chip, core, t]

        @pl.when(jnp.logical_and(inside, is_mine))
        def _():
            copy(mine, at)

        @pl.when(jnp.logical_and(inside, jnp.logical_not(is_mine)))
        def _():
            copy(theirs, jnp.where(at < 0, at + 2, at - 4))

        @pl.when(jnp.logical_not(inside))
        def _():
            for dev in range(8):
                for t in range(2 * arrays):
                    joined[j, t, 8 * dev:8 * dev + 8, :] = zero


def unpack_rows(joined, tile, dst):
    z = lanes((MX, 128)) % 2 == 0

    def part(j):
        for k in range(2):
            for a in range(2):
                v = joined[j, tile + k, pl.ds(a, MX, stride=2), :]
                y = j * 8 + 4 * k + 2 * a
                dst[y] = jnp.where(z, v, down(v, 1, 1))
                dst[y + 1] = jnp.where(z, up(v, 1, 1), v)

    rows(0, 5, part, 1)


def coarse(mid, low, rhs, m1, m2, res, lrhs, l1, l2, tmp, shrink):
    k = shrink

    def first(y):
        m1[y] = mid.inv[y] * rhs[y]

    rows(2 + 2 * k, 38 - 2 * k, first)
    mid.sweep(m2, m1, rhs, 3 + 2 * k, 37 - 2 * k)
    restrict_low(lambda y: mid.residual(m2, rhs, y), tmp, lrhs, 2 + k, 18 - k)

    def low_first(y):
        l1[y] = low.inv[y] * lrhs[y]

    rows(2 + k, 18 - k, low_first)
    low.sweep(l2, l1, lrhs, 3 + k, 17 - k)
    low.sweep(l1, l2, lrhs, 4 + k, 16 - k)
    low.sweep(l2, l1, lrhs, 5 + k, 15 - k)

    def add(i):
        v = l2[i]
        for y in (2 * i, 2 * i + 1):
            for a in range(2):
                at = pl.ds(a, LX, stride=2)
                m2[y, at, :] = m2[y, at, :] + v

    rows(5 + k, 15 - k, add, 1)
    mid.sweep(m1, m2, rhs, 11 + 2 * k, 29 - 2 * k)
    mid.sweep(m2, m1, rhs, 12 + 2 * k, 28 - 2 * k)


def prolong_add(scal, m2, wide, u_ref, dst, lo, hi):
    begin = pl.multiple_of(scal[4] * 8, 8)
    zero = jnp.zeros((8, 128), F32)

    def body(m):
        v = m2[m]
        wide[m, 0:8, :] = zero
        wide[m, 72:80, :] = zero
        wide[m, pl.ds(8, MX, stride=2), :] = v
        wide[m, pl.ds(9, MX, stride=2), :] = v

    rows(lo, hi, body)

    def add(m):
        w = wide[m, pl.ds(begin, FX), :]
        for y in (2 * m - 32 + HALO, 2 * m - 31 + HALO):
            dst[y] = u_ref[y] + w

    rows(lo, hi, add)


def middle_kernel(scal, src, fbx, fby, fbz, fdiag, finv, u2, mine, theirs,
                  mbx, mby, mbz, mdiag, minv, lbx, lby, lbz, linv, u2_out, pack,
                  joined, rhs, absorb, conduct, m1, m2, lrhs, l1, l2, labsorb, lconduct, tmp, wide, fa, fb):
    fine = Level(fbx, fby, fbz, fdiag, finv, 1)
    mid = Level(mbx, mby, mbz, mdiag, minv, 2)
    low = Level(lbx, lby, lbz, None, linv, 4)
    gather_rows(scal, mine, theirs, joined, 3)
    unpack_rows(joined, 0, rhs)
    unpack_rows(joined, 2, absorb)
    unpack_rows(joined, 4, conduct)
    mid.build(conduct, absorb, 2, 38, 4.0, True)
    restrict_low(lambda y: absorb[y], tmp, labsorb, 1, 19)
    restrict_low(lambda y: conduct[y], tmp, lconduct, 1, 19)
    low.build(lconduct, labsorb, 2, 18, 16.0, True)
    coarse(mid, low, rhs, m1, m2, None, lrhs, l1, l2, tmp, 0)
    prolong_add(scal, m2, wide, u2, fa, 12, 28)
    fine.sweep(fb, fa, src, 3, ROWS - 3)
    fine.sweep(fa, fb, src, 4, ROWS - 4)
    fine.sweep(fb, fa, src, 5, ROWS - 5)
    zero = jnp.zeros((FX, 128), F32)
    for y in (*range(6), *range(ROWS - 6, ROWS)):
        u2_out[y] = zero
    fine.sweep(u2_out, fb, src, 6, ROWS - 6)
    tiles = restrict_own(lambda i: fine.residual(u2_out, src, HALO + i)[8:16])
    for i, t in enumerate(tiles):
        pack[i] = t


def last_kernel(scal, src, fbx, fby, fbz, fdiag, finv, u2, mine, theirs,
                mbx, mby, mbz, mdiag, minv, lbx, lby, lbz, linv,
                out, out_res,
                joined, rhs, m1, m2, lrhs, l1, l2, tmp, wide, fa, fb):
    fine = Level(fbx, fby, fbz, fdiag, finv, 1)
    mid = Level(mbx, mby, mbz, mdiag, minv, 2)
    low = Level(lbx, lby, lbz, None, linv, 4)
    gather_rows(scal, mine, theirs, joined, 1)
    unpack_rows(joined, 0, rhs)
    coarse(mid, low, rhs, m1, m2, None, lrhs, l1, l2, tmp, 1)
    prolong_add(scal, m2, wide, u2, fa, 14, 26)
    fine.sweep(fb, fa, src, 7, ROWS - 7)
    fine.sweep(fa, fb, src, 8, ROWS - 8)

    def finish(y):
        at = pl.ds(y, 8, stride=16)
        out[at, :] = fa[HALO + y, 8:16, :]
        out_res[at, :] = fine.residual(fa, src, HALO + y)[8:16]

    rows(0, 16, finish)


def call(kernel, outs, scratch, *args):
    return pl.pallas_call(
        kernel,
        out_shape=[jax.ShapeDtypeStruct(s, F32) for s in outs],
        in_specs=[pl.BlockSpec(memory_space=pltpu.SMEM)]
        + [pl.BlockSpec(memory_space=pltpu.VMEM)] * (len(args) - 1),
        out_specs=[pl.BlockSpec(memory_space=pltpu.VMEM)] * len(outs),
        scratch_shapes=[pltpu.VMEM(s, F32) for s in scratch],
        compiler_params=pltpu.CompilerParams(vmem_limit_bytes=VMEM_LIMIT),
    )(*args)


def other_core(array):
    return lax.ppermute(array, "dev", [(i, i ^ 1) for i in range(8)])


def spread(pack, core, pos, groups):
    partner = other_core(pack)
    first = core == 0
    pair = jnp.stack([jnp.where(first, pack, partner), jnp.where(first, partner, pack)])
    mine = lax.all_to_all(jnp.broadcast_to(pair, (16,) + pair.shape), ("grp", "dev"), 0, 0, axis_index_groups=groups)
    theirs = other_core(jnp.where(pos < 2, mine[8:], mine[:8]))
    return mine, theirs


def local(source, absorb, conduct):
    peers = lax.axis_size("grp")
    g, d = lax.axis_index("grp"), lax.axis_index("dev")
    core, chip = d % 2, d // 2
    pos = (g + 2 * core) % 4
    scal = jnp.stack([core, pos, g, jnp.int32(peers), d]).astype(jnp.int32)
    groups = [[(4 * b + p) % peers * 8 + 2 * c for p in range(4) for c in range(4)] for b in range(peers // 4)]
    groups += [[(4 * b + 2 + p) % peers * 8 + 2 * c + 1 for p in range(4) for c in range(4)] for b in range(peers // 4)]

    fine = jnp.stack([source, absorb, conduct]).transpose(0, 2, 1, 3)
    ahead = [(i, i + 1) for i in range(peers - 1)]
    back = [(j, i) for i, j in ahead]
    before = lax.ppermute(fine[:, 16 - HALO:], "grp", ahead)
    after = lax.ppermute(fine[:, :HALO], "grp", back)
    fine = jnp.concatenate([before, fine, after], axis=1)
    via_b = lax.ppermute(fine, "dev", [(1, 2), (2, 1), (3, 4), (4, 3), (5, 6), (6, 5)])
    ends = jnp.stack([fine[2, :, 0], fine[2, :, 7]])
    via_c = lax.ppermute(ends, "dev", [(0, 2), (2, 0), (1, 3), (3, 1), (4, 6), (6, 4), (5, 7), (7, 5)])
    via_d = lax.ppermute(ends, "dev", [(2, 4), (4, 2), (3, 5), (5, 3)])
    via_a = other_core(fine)
    edge_r = jnp.where(chip % 2 == 0, via_c[0], via_d[0])
    edge_l = jnp.where(chip % 2 == 0, via_d[1], via_c[1])

    block, wide_mid, wide_low = (ROWS, FX, 128), (MROWS, MX, 128), (LROWS, LX, 128)
    *state, pack = call(
        fine_kernel, [block] * 7 + [(6, 8, 128)], [block] * 3, scal, fine, via_a, via_b, edge_l, edge_r
    )
    mine, theirs = spread(pack, core, pos, groups)
    *coefs, u2, pack = call(
        middle_kernel,
        [wide_mid] * 5 + [wide_low] * 4 + [block, (2, 8, 128)],
        [(5, 6, 64, 128)] + [wide_mid] * 5 + [wide_low] * 5 + [(MX, 128), (MROWS, 80, 128), block, block],
        scal, *state, mine, theirs,
    )
    mine, theirs = spread(pack, core, pos, groups)
    out, res = call(
        last_kernel,
        [(128, 128), (128, 128)],
        [(5, 2, 64, 128)] + [wide_mid] * 3 + [wide_low] * 3 + [(MX, 128), (MROWS, 80, 128), block, block],
        scal, *state[:6], u2, mine, theirs, *coefs,
    )
    return out.reshape(8, 16, 128), res.reshape(8, 16, 128)


def solution(mesh):
    spec = P("dev", "grp", None)
    return jax.shard_map(local, mesh=mesh, in_specs=(spec,) * 3, out_specs=(spec,) * 2, check_vma=False)
```

```python
import functools

import jax
import jax.numpy as jnp
from jax import lax
from jax.experimental import pallas as pl
from jax.experimental.pallas import tpu as pltpu
from jax.sharding import PartitionSpec as P

RELAX = 0.8
HALO = 9
ROWS = 16 + 2 * HALO
FX = 24
MROWS = 40
MX = 32
LROWS = 20
LX = 16
VMEM_LIMIT = 40 * 1024 * 1024

F32 = jnp.float32


def rows(lo, hi, body):
    body(lo, hi - lo)


def lanes(shape):
    return lax.broadcasted_iota(jnp.int32, shape, 1)


def planes(shape):
    return lax.broadcasted_iota(jnp.int32, shape, 0)


def up(value, axis, by):
    return pltpu.roll(value, value.shape[axis] - by, axis)


def down(value, axis, by):
    return pltpu.roll(value, by, axis)


class Level:
    def __init__(self, bx, by, bz, diag, inv, width):
        self.bx, self.by, self.bz, self.diag, self.inv, self.width = bx, by, bz, diag, inv, width

    def beside(self, u_ref, y, n):
        u = [u_ref[y - 1 + t] for t in range(n + 2)]
        by = [self.by[y - 1 + t] for t in range(n + 1)]
        flow = [by[t] * u[t + 1] for t in range(n + 1)]
        acc = []
        for t in range(n):
            here, bx, bz = u[t + 1], self.bx[y + t], self.bz[y + t]
            x = bx * up(here, 0, 1) + down(bx * here, 0, 1)
            z = bz * up(here, 1, self.width) + down(bz * here, 1, self.width)
            acc.append((by[t] * u[t] + by[t + 1] * u[t + 2]) + (x + z))
        return u[1:-1], acc

    def sweep(self, dst, src, rhs, lo, hi):
        def body(y, n):
            u, acc = self.beside(src, y, n)
            new = [(1.0 - RELAX) * u[t] + self.inv[y + t] * (rhs[y + t] + acc[t]) for t in range(n)]
            for t in range(n):
                dst[y + t] = new[t]

        rows(lo, hi, body)

    def residual(self, u_ref, rhs, y, n):
        u, acc = self.beside(u_ref, y, n)
        return [rhs[y + t] - self.diag[y + t] * u[t] + acc[t] for t in range(n)]

    def build(self, conduct, absorb, lo, hi, spacing, closed):
        shape = conduct.shape[1:]
        z, x = lanes(shape), planes(shape)
        half = 0.5 / spacing

        def body(y, n):
            c = [conduct[y - 1 + t] for t in range(n + 2)]
            done = []
            for t in range(n):
                here = c[t + 1]
                xp, xm = up(here, 0, 1), down(here, 0, 1)
                if closed:
                    xp = jnp.where(x == shape[0] - 1, 0.0, xp)
                    xm = jnp.where(x == 0, 0.0, xm)
                zp = jnp.where(z >= shape[1] - self.width, 0.0, up(here, 1, self.width))
                zm = jnp.where(z < self.width, 0.0, down(here, 1, self.width))
                bx = (here + xp) * half
                if closed:
                    bx = jnp.where(x == shape[0] - 1, 0.0, bx)
                by = (here + c[t + 2]) * half
                bz = jnp.where(z >= shape[1] - self.width, 0.0, (here + zp) * half)
                a = absorb[y + t]
                diag = a + (3.0 / spacing) * here + half * (((xp + xm) + (c[t] + c[t + 2])) + (zp + zm))
                done.append((bx, by, bz, diag, jnp.where(a > 0.0, RELAX / diag, 0.0)))
            for t in range(n):
                for ref, value in zip((self.bx, self.by, self.bz, self.diag, self.inv), done[t]):
                    if ref is not None:
                        ref[y + t] = value

        self.by[lo - 1] = (conduct[lo - 1] + conduct[lo]) * half
        rows(lo, hi, body)


def pair_lanes(t, width):
    first = (lanes(t.shape) // width) % 2 == 0
    return t + jnp.where(first, up(t, 1, width), down(t, 1, width))


def pair_planes(t):
    first = planes(t.shape) % 2 == 0
    return t + jnp.where(first, up(t, 0, 1), down(t, 0, 1))


def pack_rows(row_of):
    x, z = planes((8, 128)) % 2, lanes((8, 128)) % 2
    tiles = []
    for k in range(2):
        r = [row_of(4 * k + t) for t in range(4)]
        tiles.append(jnp.where(x == 0, jnp.where(z == 0, r[0], r[1]), jnp.where(z == 0, r[2], r[3])))
    return tiles


def restrict_own(r):
    def row_of(j):
        return pair_planes(pair_lanes(r[2 * j] + r[2 * j + 1], 1)) * 0.125

    return pack_rows(row_of)


def restrict_low(fine_rows, tmp, dst, lo, hi):
    def body(i, n):
        r = fine_rows(2 * i, 2 * n)
        for t in range(n):
            tmp[t] = pair_lanes(r[2 * t] + r[2 * t + 1], 2)
        for t in range(n):
            dst[i + t] = (tmp[t, pl.ds(0, LX, stride=2), :] + tmp[t, pl.ds(1, LX, stride=2), :]) * 0.125

    rows(lo, hi, body)


def scale(dst, factor, src, lo, hi):
    def body(y, n):
        new = [factor[y + t] * src[y + t] for t in range(n)]
        for t in range(n):
            dst[y + t] = new[t]

    rows(lo, hi, body)


def fine_kernel(scal, own, via_a, via_b,
                src, bx, by, bz, diag, inv, u1, pack, ends,
                absorb, conduct, u2):
    even = scal[0] == 0

    def join(y, n):
        for t in range(n):
            for arr, dst in ((0, src), (1, absorb), (2, conduct)):
                a, b = via_a[arr, y + t], via_b[arr, y + t]
                dst[y + t, 0:8, :] = jnp.where(even, b, a)
                dst[y + t, 8:16, :] = own[arr, y + t]
                dst[y + t, 16:24, :] = jnp.where(even, a, b)

    rows(0, ROWS, join)
    level = Level(bx, by, bz, diag, inv, 1)
    level.build(conduct, absorb, 1, ROWS - 1, 1.0, False)
    scale(u1, inv, src, 1, ROWS - 1)
    for y in range(1, ROWS - 1):
        for i, x in enumerate((8, 15)):
            ends[i, y - 1:y, :] = u1[y, x:x + 1, :]
    level.sweep(u2, u1, src, HALO - 1, ROWS - HALO + 1)
    tiles = restrict_own([r[8:16] for r in level.residual(u2, src, HALO, 16)])
    tiles += restrict_own([absorb[HALO + i, 8:16, :] for i in range(16)])
    tiles += restrict_own([conduct[HALO + i, 8:16, :] for i in range(16)])
    for i, t in enumerate(tiles):
        pack[i] = t


def gather_rows(scal, here, near, swapped, joined, arrays):
    even = scal[0] == 0

    def copy(j, source):
        for t in range(2 * arrays):
            for dev in range(8):
                joined[j, t, 8 * dev:8 * dev + 8, :] = source[dev, t]

    copy(2, here)
    for i in range(2):
        after, before = 3 + i, 1 - i

        @pl.when(even)
        def _():
            copy(after, near.at[i])
            copy(before, swapped.at[i])

        @pl.when(jnp.logical_not(even))
        def _():
            copy(after, swapped.at[i])
            copy(before, near.at[i])


def unpack_rows(joined, tile, dst):
    z = lanes((MX, 128)) % 2 == 0

    for j in range(5):
        for k in range(2):
            for a in range(2):
                v = joined[j, tile + k, pl.ds(a, MX, stride=2), :]
                y = j * 8 + 4 * k + 2 * a
                dst[y] = jnp.where(z, v, down(v, 1, 1))
                dst[y + 1] = jnp.where(z, up(v, 1, 1), v)


def coarse(mid, low, rhs, m1, m2, lrhs, l1, l2, tmp, k):
    scale(m1, mid.inv, rhs, 2 + 2 * k, 38 - 2 * k)
    mid.sweep(m2, m1, rhs, 3 + 2 * k, 37 - 2 * k)
    restrict_low(functools.partial(mid.residual, m2, rhs), tmp, lrhs, 2 + k, 18 - k)
    scale(l1, low.inv, lrhs, 2 + k, 18 - k)
    low.sweep(l2, l1, lrhs, 3 + k, 17 - k)
    low.sweep(l1, l2, lrhs, 4 + k, 16 - k)
    low.sweep(l2, l1, lrhs, 5 + k, 15 - k)

    for i in range(5 + k, 15 - k):
        v = l2[i]
        for y in (2 * i, 2 * i + 1):
            for a in range(2):
                at = pl.ds(a, LX, stride=2)
                m2[y, at, :] = m2[y, at, :] + v

    mid.sweep(m1, m2, rhs, 11 + 2 * k, 29 - 2 * k)
    mid.sweep(m2, m1, rhs, 12 + 2 * k, 28 - 2 * k)


def prolong_add(scal, m2, wide, u_ref, dst, lo, hi):
    begin = pl.multiple_of(scal[1] * 8, 8)
    zero = jnp.zeros((8, 128), F32)

    def body(m, n):
        for t in range(n):
            v = m2[m + t]
            wide[m + t, 0:8, :] = zero
            wide[m + t, 72:80, :] = zero
            wide[m + t, pl.ds(8, MX, stride=2), :] = v
            wide[m + t, pl.ds(9, MX, stride=2), :] = v

    rows(lo, hi, body)

    def add(m, n):
        y = 2 * m - 32 + HALO
        new = []
        for t in range(n):
            w = wide[m + t, pl.ds(begin, FX), :]
            new += [u_ref[y + 2 * t] + w, u_ref[y + 2 * t + 1] + w]
        for t in range(2 * n):
            dst[y + t] = new[t]

    rows(lo, hi, add)


def middle_kernel(scal, src, fbx, fby, fbz, fdiag, finv, u1, ends, here, near, swapped,
                  mbx, mby, mbz, mdiag, minv, lbx, lby, lbz, linv, u2_out, pack,
                  joined, rhs, absorb, conduct, m1, m2, lrhs, l1, l2, labsorb, lconduct, tmp, wide, fa, fb):
    fine = Level(fbx, fby, fbz, fdiag, finv, 1)
    mid = Level(mbx, mby, mbz, mdiag, minv, 2)
    low = Level(lbx, lby, lbz, None, linv, 4)
    gather_rows(scal, here, near, swapped, joined, 3)
    unpack_rows(joined, 0, rhs)
    unpack_rows(joined, 2, absorb)
    unpack_rows(joined, 4, conduct)
    mid.build(conduct, absorb, 2, 38, 4.0, True)
    restrict_low(lambda y, n: [absorb[y + t] for t in range(n)], tmp, labsorb, 1, 19)
    restrict_low(lambda y, n: [conduct[y + t] for t in range(n)], tmp, lconduct, 1, 19)
    low.build(lconduct, labsorb, 2, 18, 16.0, True)
    coarse(mid, low, rhs, m1, m2, lrhs, l1, l2, tmp, 0)
    x = planes((FX, 128))
    dev = scal[1]
    left, right = jnp.maximum(dev - 1, 0), jnp.minimum(dev + 1, 7)

    def first(y, n):
        new = []
        for t in range(n):
            at = pl.ds(y + t - 1, 1)
            u = jnp.where(x == 0, ends[left, at, :], jnp.where(x == FX - 1, ends[right, at, :], u1[y + t]))
            new.append(u)
        for t in range(n):
            fa[y + t] = new[t]

    rows(1, ROWS - 1, first)
    zero = jnp.zeros((FX, 128), F32)
    for y in (0, 1, ROWS - 2, ROWS - 1):
        fb[y] = zero
    fine.sweep(fb, fa, src, 2, ROWS - 2)
    prolong_add(scal, m2, wide, fb, fa, 12, 28)
    fine.sweep(fb, fa, src, 3, ROWS - 3)
    fine.sweep(fa, fb, src, 4, ROWS - 4)
    fine.sweep(fb, fa, src, 5, ROWS - 5)
    for y in (*range(6), *range(ROWS - 6, ROWS)):
        u2_out[y] = zero
    fine.sweep(u2_out, fb, src, 6, ROWS - 6)
    tiles = restrict_own([r[8:16] for r in fine.residual(u2_out, src, HALO, 16)])
    for i, t in enumerate(tiles):
        pack[i] = t


def last_kernel(scal, src, fbx, fby, fbz, fdiag, finv, u2, here, near, swapped,
                mbx, mby, mbz, mdiag, minv, lbx, lby, lbz, linv,
                out, out_res,
                joined, rhs, m1, m2, lrhs, l1, l2, tmp, wide, fa, fb):
    fine = Level(fbx, fby, fbz, fdiag, finv, 1)
    mid = Level(mbx, mby, mbz, mdiag, minv, 2)
    low = Level(lbx, lby, lbz, None, linv, 4)
    gather_rows(scal, here, near, swapped, joined, 1)
    unpack_rows(joined, 0, rhs)
    coarse(mid, low, rhs, m1, m2, lrhs, l1, l2, tmp, 1)
    prolong_add(scal, m2, wide, u2, fa, 14, 26)
    fine.sweep(fb, fa, src, 7, ROWS - 7)
    fine.sweep(fa, fb, src, 8, ROWS - 8)

    def finish(y, n):
        r = fine.residual(fa, src, HALO + y, n)
        for t in range(n):
            at = pl.ds(y + t, 8, stride=16)
            out[at, :] = fa[HALO + y + t, 8:16, :]
            out_res[at, :] = r[t][8:16]

    rows(0, 16, finish)


def call(kernel, outs, scratch, *args):
    return pl.pallas_call(
        kernel,
        out_shape=[jax.ShapeDtypeStruct(s, F32) for s in outs],
        in_specs=[pl.BlockSpec(memory_space=pltpu.SMEM)]
        + [pl.BlockSpec(memory_space=pltpu.VMEM)] * (len(args) - 1),
        out_specs=[pl.BlockSpec(memory_space=pltpu.VMEM)] * len(outs),
        scratch_shapes=[pltpu.VMEM(s, F32) for s in scratch],
        compiler_params=pltpu.CompilerParams(vmem_limit_bytes=VMEM_LIMIT),
    )(*args)


def other_core(array):
    return lax.ppermute(array, "dev", [(i, i ^ 1) for i in range(8)])


def spread(pack, ends=None):
    peers, devs = lax.axis_size("grp"), lax.axis_size("dev")

    def from_beside(array, by):
        pairs = []
        for g in range(peers):
            for d in range(devs):
                there = g + by if d % 2 == 0 else g - by
                if 0 <= there < peers:
                    pairs.append((there * devs + d, g * devs + d))
        return lax.ppermute(array, ("grp", "dev"), pairs)

    here = jnp.broadcast_to(pack, (devs,) + pack.shape)
    if ends is not None:
        d = lax.axis_index("dev")
        mine = jnp.where(jnp.arange(devs)[:, None, None] < d, ends[0], ends[1])
        here = jnp.concatenate([here, mine.reshape(devs, 4, 8, 128)], axis=1)
    here = lax.all_to_all(here, "dev", 0, 0)
    if ends is not None:
        ends = here[:, -4:].reshape(devs, 32, 128)
        here = here[:, :-4]
    near = jnp.stack([from_beside(here, 1), from_beside(here, 2)])
    return ends, here, near, other_core(near)


def local(source, absorb, conduct):
    peers = lax.axis_size("grp")
    d = lax.axis_index("dev")
    scal = jnp.stack([d % 2, d]).astype(jnp.int32)

    fine = jnp.stack([source, absorb, conduct]).transpose(0, 2, 1, 3)
    ahead = [(i, i + 1) for i in range(peers - 1)]
    back = [(j, i) for i, j in ahead]
    args = (source, absorb, conduct)
    before = lax.ppermute(jnp.stack([a[:, 16 - HALO:].transpose(1, 0, 2) for a in args]), "grp", ahead)
    after = lax.ppermute(jnp.stack([a[:, :HALO].transpose(1, 0, 2) for a in args]), "grp", back)
    fine = jnp.concatenate([before, fine, after], axis=1)
    via_b = lax.ppermute(fine, "dev", [(1, 2), (2, 1), (3, 4), (4, 3), (5, 6), (6, 5)])
    via_a = other_core(fine)
    block, wide_mid, wide_low = (ROWS, FX, 128), (MROWS, MX, 128), (LROWS, LX, 128)
    *state, u1, pack, ends = call(
        fine_kernel, [block] * 7 + [(6, 8, 128), (2, 32, 128)], [block] * 3, scal, fine, via_a, via_b
    )
    ends, *parts = spread(pack, ends)
    *coefs, u2, pack = call(
        middle_kernel,
        [wide_mid] * 5 + [wide_low] * 4 + [block, (2, 8, 128)],
        [(5, 6, 64, 128)] + [wide_mid] * 5 + [wide_low] * 5 + [(20, MX, 128), (MROWS, 80, 128), block, block],
        scal, *state, u1, ends, *parts,
    )
    _, *parts = spread(pack)
    out, res = call(
        last_kernel,
        [(128, 128), (128, 128)],
        [(5, 2, 64, 128)] + [wide_mid] * 3 + [wide_low] * 3 + [(20, MX, 128), (MROWS, 80, 128), block, block],
        scal, *state, u2, *parts, *coefs,
    )
    return out.reshape(8, 16, 128), res.reshape(8, 16, 128)


def solution(mesh):
    spec = P("dev", "grp", None)
    return jax.shard_map(local, mesh=mesh, in_specs=(spec,) * 3, out_specs=(spec,) * 2, check_vma=False)
```

```python
import functools

import jax
import jax.numpy as jnp
from jax import lax
from jax.experimental import pallas as pl
from jax.experimental.pallas import tpu as pltpu
from jax.sharding import PartitionSpec as P

RELAX = 0.8
HALO = 9
ROWS = 16 + 2 * HALO
FX = 24
MROWS = 40
MX = 32
LROWS = 20
LX = 16
VMEM_LIMIT = 40 * 1024 * 1024

F32 = jnp.float32


def rows(lo, hi, body):
    body(lo, hi - lo)


def lanes(shape):
    return lax.broadcasted_iota(jnp.int32, shape, 1)


def planes(shape):
    return lax.broadcasted_iota(jnp.int32, shape, 0)


def up(value, axis, by):
    return pltpu.roll(value, value.shape[axis] - by, axis)


def down(value, axis, by):
    return pltpu.roll(value, by, axis)


class Level:
    def __init__(self, bx, by, bz, diag, inv, width):
        self.bx, self.by, self.bz, self.diag, self.inv, self.width = bx, by, bz, diag, inv, width

    def beside(self, u_ref, y, n):
        u = [u_ref[y - 1 + t] for t in range(n + 2)]
        by = [self.by[y - 1 + t] for t in range(n + 1)]
        flow = [by[t] * u[t + 1] for t in range(n + 1)]
        acc = []
        for t in range(n):
            here, bx, bz = u[t + 1], self.bx[y + t], self.bz[y + t]
            x = bx * up(here, 0, 1) + down(bx * here, 0, 1)
            z = bz * up(here, 1, self.width) + down(bz * here, 1, self.width)
            acc.append((by[t] * u[t] + by[t + 1] * u[t + 2]) + (x + z))
        return u[1:-1], acc

    def sweep(self, dst, src, rhs, lo, hi):
        def body(y, n):
            u, acc = self.beside(src, y, n)
            new = [(1.0 - RELAX) * u[t] + self.inv[y + t] * (rhs[y + t] + acc[t]) for t in range(n)]
            for t in range(n):
                dst[y + t] = new[t]

        rows(lo, hi, body)

    def residual(self, u_ref, rhs, y, n):
        u, acc = self.beside(u_ref, y, n)
        return [rhs[y + t] - self.diag[y + t] * u[t] + acc[t] for t in range(n)]

    def build(self, conduct, absorb, lo, hi, spacing, closed):
        shape = conduct.shape[1:]
        z, x = lanes(shape), planes(shape)
        half = 0.5 / spacing

        def body(y, n):
            c = [conduct[y - 1 + t] for t in range(n + 2)]
            done = []
            for t in range(n):
                here = c[t + 1]
                xp, xm = up(here, 0, 1), down(here, 0, 1)
                if closed:
                    xp = jnp.where(x == shape[0] - 1, 0.0, xp)
                    xm = jnp.where(x == 0, 0.0, xm)
                zp = jnp.where(z >= shape[1] - self.width, 0.0, up(here, 1, self.width))
                zm = jnp.where(z < self.width, 0.0, down(here, 1, self.width))
                bx = (here + xp) * half
                if closed:
                    bx = jnp.where(x == shape[0] - 1, 0.0, bx)
                by = (here + c[t + 2]) * half
                bz = jnp.where(z >= shape[1] - self.width, 0.0, (here + zp) * half)
                a = absorb[y + t]
                diag = a + (3.0 / spacing) * here + half * (((xp + xm) + (c[t] + c[t + 2])) + (zp + zm))
                done.append((bx, by, bz, diag, jnp.where(a > 0.0, RELAX / diag, 0.0)))
            for t in range(n):
                for ref, value in zip((self.bx, self.by, self.bz, self.diag, self.inv), done[t]):
                    if ref is not None:
                        ref[y + t] = value

        self.by[lo - 1] = (conduct[lo - 1] + conduct[lo]) * half
        rows(lo, hi, body)


def pair_lanes(t, width):
    first = (lanes(t.shape) // width) % 2 == 0
    return t + jnp.where(first, up(t, 1, width), down(t, 1, width))


def pair_planes(t):
    first = planes(t.shape) % 2 == 0
    return t + jnp.where(first, up(t, 0, 1), down(t, 0, 1))


def pack_rows(row_of):
    x, z = planes((8, 128)) % 2, lanes((8, 128)) % 2
    tiles = []
    for k in range(2):
        r = [row_of(4 * k + t) for t in range(4)]
        tiles.append(jnp.where(x == 0, jnp.where(z == 0, r[0], r[1]), jnp.where(z == 0, r[2], r[3])))
    return tiles


def restrict_own(r):
    def row_of(j):
        return pair_planes(pair_lanes(r[2 * j] + r[2 * j + 1], 1)) * 0.125

    return pack_rows(row_of)


def restrict_low(fine_rows, tmp, dst, lo, hi):
    def body(i, n):
        r = fine_rows(2 * i, 2 * n)
        for t in range(n):
            tmp[t] = r[2 * t] + r[2 * t + 1]
        for t in range(n):
            pair = tmp[t, pl.ds(0, LX, stride=2), :] + tmp[t, pl.ds(1, LX, stride=2), :]
            dst[i + t] = pair_lanes(pair, 2) * 0.125

    rows(lo, hi, body)


def scale(dst, factor, src, lo, hi):
    def body(y, n):
        new = [factor[y + t] * src[y + t] for t in range(n)]
        for t in range(n):
            dst[y + t] = new[t]

    rows(lo, hi, body)


def fine_kernel(scal, own, via_a, via_b,
                src, bx, by, bz, diag, inv, u1, pack, ends,
                absorb, conduct, u2):
    even = scal[0] == 0

    def join(y, n):
        for t in range(n):
            for arr, dst in ((0, src), (1, absorb), (2, conduct)):
                a, b = via_a[arr, y + t], via_b[arr, y + t]
                dst[y + t, 0:8, :] = jnp.where(even, b, a)
                dst[y + t, 8:16, :] = own[arr, y + t]
                dst[y + t, 16:24, :] = jnp.where(even, a, b)

    rows(0, ROWS, join)
    level = Level(bx, by, bz, diag, inv, 1)
    level.build(conduct, absorb, 1, ROWS - 1, 1.0, False)
    scale(u1, inv, src, 1, ROWS - 1)
    for y in range(16):
        for i, x in enumerate((8, 15)):
            ends[i, y:y + 1, :] = u1[HALO + y, x:x + 1, :]
    level.sweep(u2, u1, src, HALO - 1, ROWS - HALO + 1)
    tiles = restrict_own([r[8:16] for r in level.residual(u2, src, HALO, 16)])
    tiles += restrict_own([absorb[HALO + i, 8:16, :] for i in range(16)])
    tiles += restrict_own([conduct[HALO + i, 8:16, :] for i in range(16)])
    for i, t in enumerate(tiles):
        pack[i] = t


def gather_rows(scal, here, near, swapped, joined, arrays):
    def copy(j, source):
        for t in range(2 * arrays):
            for dev in range(8):
                joined[j, t, 8 * dev:8 * dev + 8, :] = source[dev, t]

    copy(2, here)
    for i in range(2):
        after, before = 3 + i, 1 - i
        near_after = scal[2 + i] != 0

        @pl.when(near_after)
        def _():
            copy(after, near.at[i])
            copy(before, swapped.at[i])

        @pl.when(jnp.logical_not(near_after))
        def _():
            copy(after, swapped.at[i])
            copy(before, near.at[i])


def unpack_rows(joined, tile, dst):
    z = lanes((MX, 128)) % 2 == 0

    for j in range(5):
        for k in range(2):
            for a in range(2):
                v = joined[j, tile + k, pl.ds(a, MX, stride=2), :]
                y = j * 8 + 4 * k + 2 * a
                dst[y] = jnp.where(z, v, down(v, 1, 1))
                dst[y + 1] = jnp.where(z, up(v, 1, 1), v)


def coarse(mid, low, rhs, m1, m2, lrhs, l1, l2, tmp, k):
    scale(m1, mid.inv, rhs, 2 + 2 * k, 38 - 2 * k)
    mid.sweep(m2, m1, rhs, 3 + 2 * k, 37 - 2 * k)
    restrict_low(functools.partial(mid.residual, m2, rhs), tmp, lrhs, 2 + k, 18 - k)
    scale(l1, low.inv, lrhs, 2 + k, 18 - k)
    low.sweep(l2, l1, lrhs, 3 + k, 17 - k)
    low.sweep(l1, l2, lrhs, 4 + k, 16 - k)
    low.sweep(l2, l1, lrhs, 5 + k, 15 - k)

    for i in range(5 + k, 15 - k):
        v = l2[i]
        for y in (2 * i, 2 * i + 1):
            for a in range(2):
                at = pl.ds(a, LX, stride=2)
                m2[y, at, :] = m2[y, at, :] + v

    mid.sweep(m1, m2, rhs, 11 + 2 * k, 29 - 2 * k)
    mid.sweep(m2, m1, rhs, 12 + 2 * k, 28 - 2 * k)


def prolong_add(scal, m2, wide, u_ref, dst, lo, hi):
    begin = pl.multiple_of(scal[1] * 8, 8)
    zero = jnp.zeros((8, 128), F32)

    def body(m, n):
        for t in range(n):
            v = m2[m + t]
            wide[m + t, 0:8, :] = zero
            wide[m + t, 72:80, :] = zero
            wide[m + t, pl.ds(8, MX, stride=2), :] = v
            wide[m + t, pl.ds(9, MX, stride=2), :] = v

    rows(lo, hi, body)

    def add(m, n):
        y = 2 * m - 32 + HALO
        new = []
        for t in range(n):
            w = wide[m + t, pl.ds(begin, FX), :]
            new += [u_ref[y + 2 * t] + w, u_ref[y + 2 * t + 1] + w]
        for t in range(2 * n):
            dst[y + t] = new[t]

    rows(lo, hi, add)


def middle_kernel(scal, src, fbx, fby, fbz, fdiag, finv, u1, ends, here, near, swapped,
                  mbx, mby, mbz, mdiag, minv, lbx, lby, lbz, linv, u2_out, pack,
                  joined, rhs, absorb, conduct, m1, m2, lrhs, l1, l2, labsorb, lconduct, tmp, wide, fa, fb):
    fine = Level(fbx, fby, fbz, fdiag, finv, 1)
    mid = Level(mbx, mby, mbz, mdiag, minv, 2)
    low = Level(lbx, lby, lbz, None, linv, 4)
    gather_rows(scal, here, near, swapped, joined, 3)
    unpack_rows(joined, 0, rhs)
    unpack_rows(joined, 2, absorb)
    unpack_rows(joined, 4, conduct)
    mid.build(conduct, absorb, 2, 38, 4.0, True)
    restrict_low(lambda y, n: [absorb[y + t] for t in range(n)], tmp, labsorb, 1, 19)
    restrict_low(lambda y, n: [conduct[y + t] for t in range(n)], tmp, lconduct, 1, 19)
    low.build(lconduct, labsorb, 2, 18, 16.0, True)
    coarse(mid, low, rhs, m1, m2, lrhs, l1, l2, tmp, 0)
    x = planes((FX, 128))
    dev = scal[1]
    left, right = jnp.maximum(dev - 1, 0), jnp.minimum(dev + 1, 7)

    for y in range(1, ROWS - 1):
        u = u1[y]
        if 0 <= y - HALO < 16:
            at = pl.ds(y - HALO, 1)
            u = jnp.where(x == 0, ends[left, at, :], jnp.where(x == FX - 1, ends[right, at, :], u))
        fa[y] = u
    zero = jnp.zeros((FX, 128), F32)
    for y in (0, 1, ROWS - 2, ROWS - 1):
        fb[y] = zero
    fine.sweep(fb, fa, src, 2, ROWS - 2)
    prolong_add(scal, m2, wide, fb, fa, 12, 28)
    fine.sweep(fb, fa, src, 3, ROWS - 3)
    fine.sweep(fa, fb, src, 4, ROWS - 4)
    fine.sweep(fb, fa, src, 5, ROWS - 5)
    for y in (*range(6), *range(ROWS - 6, ROWS)):
        u2_out[y] = zero
    fine.sweep(u2_out, fb, src, 6, ROWS - 6)
    tiles = restrict_own([r[8:16] for r in fine.residual(u2_out, src, HALO, 16)])
    for i, t in enumerate(tiles):
        pack[i] = t


def last_kernel(scal, src, fbx, fby, fbz, fdiag, finv, u2, here, near, swapped,
                mbx, mby, mbz, mdiag, minv, lbx, lby, lbz, linv,
                out, out_res,
                joined, rhs, m1, m2, lrhs, l1, l2, tmp, wide, fa, fb):
    fine = Level(fbx, fby, fbz, fdiag, finv, 1)
    mid = Level(mbx, mby, mbz, mdiag, minv, 2)
    low = Level(lbx, lby, lbz, None, linv, 4)
    gather_rows(scal, here, near, swapped, joined, 1)
    unpack_rows(joined, 0, rhs)
    coarse(mid, low, rhs, m1, m2, lrhs, l1, l2, tmp, 1)
    prolong_add(scal, m2, wide, u2, fa, 14, 26)
    fine.sweep(fb, fa, src, 7, ROWS - 7)
    fine.sweep(fa, fb, src, 8, ROWS - 8)

    def finish(y, n):
        r = fine.residual(fa, src, HALO + y, n)
        for t in range(n):
            at = pl.ds(y + t, 8, stride=16)
            out[at, :] = fa[HALO + y + t, 8:16, :]
            out_res[at, :] = r[t][8:16]

    rows(0, 16, finish)


def call(kernel, outs, scratch, *args):
    return pl.pallas_call(
        kernel,
        out_shape=[jax.ShapeDtypeStruct(s, F32) for s in outs],
        in_specs=[pl.BlockSpec(memory_space=pltpu.SMEM)]
        + [pl.BlockSpec(memory_space=pltpu.VMEM)] * (len(args) - 1),
        out_specs=[pl.BlockSpec(memory_space=pltpu.VMEM)] * len(outs),
        scratch_shapes=[pltpu.VMEM(s, F32) for s in scratch],
        compiler_params=pltpu.CompilerParams(vmem_limit_bytes=VMEM_LIMIT),
    )(*args)


def other_core(array):
    return lax.ppermute(array, "dev", [(i, i ^ 1) for i in range(8)])


def one_away(g, core):
    return 1 if g % 2 == core else -1


def two_away(g, core):
    return 2 if g // 2 % 2 != core else -2


def spread(pack, ends=None):
    peers, devs = lax.axis_size("grp"), lax.axis_size("dev")

    def from_beside(array, by):
        pairs = []
        for g in range(peers):
            for d in range(devs):
                there = g + by(g, d % 2)
                if 0 <= there < peers:
                    pairs.append((there * devs + d, g * devs + d))
        return lax.ppermute(array, ("grp", "dev"), pairs)

    here = jnp.broadcast_to(pack, (devs,) + pack.shape)
    if ends is not None:
        d = lax.axis_index("dev")
        mine = jnp.where(jnp.arange(devs)[:, None, None] < d, ends[0], ends[1])
        here = jnp.concatenate([here, mine.reshape(devs, 2, 8, 128)], axis=1)
    here = lax.all_to_all(here, "dev", 0, 0)
    if ends is not None:
        ends = here[:, -2:].reshape(devs, 16, 128)
        here = here[:, :-2]
    near = jnp.stack([from_beside(here, one_away), from_beside(here, two_away)])
    return ends, here, near, other_core(near)


def local(source, absorb, conduct):
    peers = lax.axis_size("grp")
    d = lax.axis_index("dev")
    g, core = lax.axis_index("grp"), d % 2
    scal = jnp.stack([core, d, g % 2 == core, g // 2 % 2 != core]).astype(jnp.int32)

    fine = jnp.stack([source, absorb, conduct]).transpose(0, 2, 1, 3)
    even = g % 2 == 0
    first, last = fine[:, :HALO], fine[:, 16 - HALO:]

    def swap_rows(array, low):
        pairs = [(i, i + 1) for i in range(low, peers - 1, 2)]
        return lax.ppermute(array, "grp", pairs + [(j, i) for i, j in pairs])

    one = swap_rows(jnp.where(even, last, first), 0)
    two = swap_rows(jnp.where(even, first, last), 1)
    before, after = jnp.where(even, two, one), jnp.where(even, one, two)
    fine = jnp.concatenate([before, fine, after], axis=1)
    via_b = lax.ppermute(fine, "dev", [(1, 2), (2, 1), (3, 4), (4, 3), (5, 6), (6, 5)])
    via_a = other_core(fine)
    block, wide_mid, wide_low = (ROWS, FX, 128), (MROWS, MX, 128), (LROWS, LX, 128)
    *state, u1, pack, ends = call(
        fine_kernel, [block] * 7 + [(6, 8, 128), (2, 16, 128)], [block] * 3, scal, fine, via_a, via_b
    )
    ends, *parts = spread(pack, ends)
    *coefs, u2, pack = call(
        middle_kernel,
        [wide_mid] * 5 + [wide_low] * 4 + [block, (2, 8, 128)],
        [(5, 6, 64, 128)] + [wide_mid] * 5 + [wide_low] * 5 + [(20, MX, 128), (MROWS, 80, 128), block, block],
        scal, *state, u1, ends, *parts,
    )
    _, *parts = spread(pack)
    out, res = call(
        last_kernel,
        [(128, 128), (128, 128)],
        [(5, 2, 64, 128)] + [wide_mid] * 3 + [wide_low] * 3 + [(20, MX, 128), (MROWS, 80, 128), block, block],
        scal, *state, u2, *parts, *coefs,
    )
    return out.reshape(8, 16, 128), res.reshape(8, 16, 128)


def solution(mesh):
    spec = P("dev", "grp", None)
    return jax.shard_map(local, mesh=mesh, in_specs=(spec,) * 3, out_specs=(spec,) * 2, check_vma=False)
```

```python
import functools

import jax
import jax.numpy as jnp
from jax import lax
from jax.experimental import pallas as pl
from jax.experimental.pallas import tpu as pltpu
from jax.sharding import PartitionSpec as P

RELAX = 0.8
HALO = 9
ROWS = 16 + 2 * HALO
FX = 24
MROWS = 40
MX = 16
LROWS = 20
LX = 8
VMEM_LIMIT = 40 * 1024 * 1024

F32 = jnp.float32


def rows(lo, hi, body):
    body(lo, hi - lo)


def lanes(shape):
    return lax.broadcasted_iota(jnp.int32, shape, 1)


def planes(shape):
    return lax.broadcasted_iota(jnp.int32, shape, 0)


def up(value, axis, by):
    return pltpu.roll(value, value.shape[axis] - by, axis)


def down(value, axis, by):
    return pltpu.roll(value, by, axis)


def next_plane(value):
    value = up(value, 0, 1)
    last = value[-8:]
    last = jnp.where(planes((8, 128)) == 7, up(last, 1, 1), last)
    return last if value.shape[0] == 8 else jnp.concatenate([value[:-8], last])


def previous_plane(value):
    value = down(value, 0, 1)
    first = value[:8]
    first = jnp.where(planes((8, 128)) == 0, down(first, 1, 1), first)
    return first if value.shape[0] == 8 else jnp.concatenate([first, value[8:]])


class Level:
    def __init__(self, bx, by, bz, diag, inv, width, folded):
        self.bx, self.by, self.bz, self.diag, self.inv, self.width = bx, by, bz, diag, inv, width
        self.folded = folded
        self.next = next_plane if folded else lambda value: up(value, 0, 1)
        self.previous = previous_plane if folded else lambda value: down(value, 0, 1)

    def beside(self, u_ref, y, n):
        u = [u_ref[y - 1 + t] for t in range(n + 2)]
        by = [self.by[y - 1 + t] for t in range(n + 1)]
        flow = [by[t] * u[t + 1] for t in range(n + 1)]
        acc = []
        for t in range(n):
            here, bx, bz = u[t + 1], self.bx[y + t], self.bz[y + t]
            x = bx * self.next(here) + self.previous(bx * here)
            z = bz * up(here, 1, self.width) + down(bz * here, 1, self.width)
            acc.append((by[t] * u[t] + by[t + 1] * u[t + 2]) + (x + z))
        return u[1:-1], acc

    def sweep(self, dst, src, rhs, lo, hi):
        def body(y, n):
            u, acc = self.beside(src, y, n)
            new = [(1.0 - RELAX) * u[t] + self.inv[y + t] * (rhs[y + t] + acc[t]) for t in range(n)]
            for t in range(n):
                dst[y + t] = new[t]

        rows(lo, hi, body)

    def residual(self, u_ref, rhs, y, n):
        u, acc = self.beside(u_ref, y, n)
        return [rhs[y + t] - self.diag[y + t] * u[t] + acc[t] for t in range(n)]

    def build(self, conduct, absorb, lo, hi, spacing):
        shape = conduct.shape[1:]
        z, x = lanes(shape), planes(shape)
        half = 0.5 / spacing
        final = jnp.logical_and(x == shape[0] - 1, z % 2 == 1)
        initial = jnp.logical_and(x == 0, z % 2 == 0)

        def body(y, n):
            c = [conduct[y - 1 + t] for t in range(n + 2)]
            done = []
            for t in range(n):
                here = c[t + 1]
                xp, xm = self.next(here), self.previous(here)
                if self.folded:
                    xp = jnp.where(final, 0.0, xp)
                    xm = jnp.where(initial, 0.0, xm)
                zp = jnp.where(z >= shape[1] - self.width, 0.0, up(here, 1, self.width))
                zm = jnp.where(z < self.width, 0.0, down(here, 1, self.width))
                bx = (here + xp) * half
                if self.folded:
                    bx = jnp.where(final, 0.0, bx)
                by = (here + c[t + 2]) * half
                bz = jnp.where(z >= shape[1] - self.width, 0.0, (here + zp) * half)
                a = absorb[y + t]
                diag = a + (3.0 / spacing) * here + half * (((xp + xm) + (c[t] + c[t + 2])) + (zp + zm))
                done.append((bx, by, bz, diag, jnp.where(a > 0.0, RELAX / diag, 0.0)))
            for t in range(n):
                for ref, value in zip((self.bx, self.by, self.bz, self.diag, self.inv), done[t]):
                    if ref is not None:
                        ref[y + t] = value

        self.by[lo - 1] = (conduct[lo - 1] + conduct[lo]) * half
        rows(lo, hi, body)


def pair_lanes(t, width):
    first = (lanes(t.shape) // width) % 2 == 0
    return t + jnp.where(first, up(t, 1, width), down(t, 1, width))


def pair_planes(t):
    first = planes(t.shape) % 2 == 0
    return t + jnp.where(first, up(t, 0, 1), down(t, 0, 1))


def pack_rows(row_of):
    x, z = planes((8, 128)) % 2, lanes((8, 128)) % 2
    tiles = []
    for k in range(2):
        r = [row_of(4 * k + t) for t in range(4)]
        tiles.append(jnp.where(x == 0, jnp.where(z == 0, r[0], r[1]), jnp.where(z == 0, r[2], r[3])))
    return tiles


def restrict_own(r):
    def row_of(j):
        return pair_planes(pair_lanes(r[2 * j] + r[2 * j + 1], 1)) * 0.125

    return pack_rows(row_of)


def restrict_low(fine_rows, tmp, dst, lo, hi):
    def body(i, n):
        r = fine_rows(2 * i, 2 * n)
        for t in range(n):
            tmp[t] = r[2 * t] + r[2 * t + 1]
        for t in range(n):
            pair = tmp[t, pl.ds(0, LX, stride=2), :] + tmp[t, pl.ds(1, LX, stride=2), :]
            dst[i + t] = pair_lanes(pair, 2) * 0.125

    rows(lo, hi, body)


def scale(dst, factor, src, lo, hi):
    def body(y, n):
        new = [factor[y + t] * src[y + t] for t in range(n)]
        for t in range(n):
            dst[y + t] = new[t]

    rows(lo, hi, body)


def join_planes(scal, own, via_a, via_b, arr, dst, lo, hi):
    even = scal[0] == 0
    for y in range(lo, hi):
        a, b = via_a[arr, y], via_b[arr, y]
        dst[y, 0:8, :] = jnp.where(even, b, a)
        dst[y, 8:16, :] = own[arr, y]
        dst[y, 16:24, :] = jnp.where(even, a, b)


def first_kernel(scal, own, near_a, near_b, pack, ends,
                 src, absorb, conduct, bx, by, bz, diag, inv, u1, u2):
    even = scal[0] == 0
    for arr, dst in ((0, src), (1, absorb), (2, conduct)):
        for i in range(22):
            y = HALO - 3 + i
            a, b = near_a[arr, i // 2], near_b[arr, i // 2]
            left, right = jnp.where(even, b, a), jnp.where(even, a, b)
            dst[y, 0:8, :] = down(left, 0, 4) if i % 2 == 0 else left
            dst[y, 8:16, :] = own[arr, y]
            dst[y, 16:24, :] = right if i % 2 == 0 else down(right, 0, 4)
    level = Level(bx, by, bz, diag, inv, 1, False)
    level.build(conduct, absorb, HALO - 2, ROWS - HALO + 2, 1.0)
    scale(u1, inv, src, HALO - 2, ROWS - HALO + 2)
    for y in range(16):
        for i, x in enumerate((8, 15)):
            ends[i, y:y + 1, :] = u1[HALO + y, x:x + 1, :]
    level.sweep(u2, u1, src, HALO - 1, ROWS - HALO + 1)
    tiles = restrict_own([r[8:16] for r in level.residual(u2, src, HALO, 16)])
    tiles += restrict_own([absorb[HALO + i, 8:16, :] for i in range(16)])
    tiles += restrict_own([conduct[HALO + i, 8:16, :] for i in range(16)])
    for i, t in enumerate(tiles):
        pack[i] = t


def rim_kernel(scal, own, via_a, via_b, ends,
               src, bx, by, bz, diag, inv, u2,
               absorb, conduct, u1):
    for arr, dst in ((0, src), (1, absorb), (2, conduct)):
        join_planes(scal, own, via_a, via_b, arr, dst, 0, ROWS)
    level = Level(bx, by, bz, diag, inv, 1, False)
    level.build(conduct, absorb, 1, ROWS - 1, 1.0)
    x = planes((FX, 128))
    dev = scal[1]
    left, right = jnp.maximum(dev - 1, 0), jnp.minimum(dev + 1, 7)
    for y in range(1, ROWS - 1):
        u = inv[y] * src[y]
        if 0 <= y - HALO < 16:
            at = pl.ds(y - HALO, 1)
            u = jnp.where(x == 0, ends[left, at, :], jnp.where(x == FX - 1, ends[right, at, :], u))
        u1[y] = u
    zero = jnp.zeros((FX, 128), F32)
    for y in (0, 1, ROWS - 2, ROWS - 1):
        u2[y] = zero
    level.sweep(u2, u1, src, 2, ROWS - 2)


def gather_rows(scal, here, near, swapped, joined, arrays):
    def copy(j, source):
        for t in range(2 * arrays):
            for dev in range(8):
                joined[j, t, 8 * dev:8 * dev + 8, :] = source[dev, t]

    copy(2, here)
    for i in range(2):
        after, before = 3 + i, 1 - i
        near_after = scal[2 + i] != 0

        @pl.when(near_after)
        def _():
            copy(after, near.at[i])
            copy(before, swapped.at[i])

        @pl.when(jnp.logical_not(near_after))
        def _():
            copy(after, swapped.at[i])
            copy(before, near.at[i])


def unpack_rows(joined, tile, dst):
    z = lanes((MX, 128)) % 2 == 0

    for j in range(5):
        for k in range(2):
            for a in range(2):
                v = joined[j, tile + k, pl.ds(a, 2 * MX, stride=2), :]
                v, w = v[:MX], v[MX:]
                y = j * 8 + 4 * k + 2 * a
                dst[y] = jnp.where(z, v, down(w, 1, 1))
                dst[y + 1] = jnp.where(z, up(v, 1, 1), w)


def coarse(mid, low, rhs, m1, m2, lrhs, l1, l2, tmp, k):
    scale(m1, mid.inv, rhs, 2 + 2 * k, 38 - 2 * k)
    mid.sweep(m2, m1, rhs, 3 + 2 * k, 37 - 2 * k)
    restrict_low(functools.partial(mid.residual, m2, rhs), tmp, lrhs, 2 + k, 18 - k)
    scale(l1, low.inv, lrhs, 2 + k, 18 - k)
    low.sweep(l2, l1, lrhs, 3 + k, 17 - k)
    low.sweep(l1, l2, lrhs, 4 + k, 16 - k)
    low.sweep(l2, l1, lrhs, 5 + k, 15 - k)

    for i in range(5 + k, 15 - k):
        v = l2[i]
        for y in (2 * i, 2 * i + 1):
            for a in range(2):
                at = pl.ds(a, LX, stride=2)
                m2[y, at, :] = m2[y, at, :] + v

    mid.sweep(m1, m2, rhs, 11 + 2 * k, 29 - 2 * k)
    mid.sweep(m2, m1, rhs, 12 + 2 * k, 28 - 2 * k)


def prolong_add(scal, m2, wide, u_ref, dst, lo, hi):
    begin = pl.multiple_of(scal[1] * 8, 8)
    zero = jnp.zeros((8, 128), F32)
    z = lanes((MX, 128)) % 2 == 0

    def body(m, n):
        for t in range(n):
            v = m2[m + t]
            low, high = jnp.where(z, v, down(v, 1, 1)), jnp.where(z, up(v, 1, 1), v)
            wide[m + t, 0:8, :] = zero
            wide[m + t, 72:80, :] = zero
            for a in range(2):
                wide[m + t, pl.ds(8 + a, MX, stride=2), :] = low
                wide[m + t, pl.ds(40 + a, MX, stride=2), :] = high

    rows(lo, hi, body)

    def add(m, n):
        y = 2 * m - 32 + HALO
        new = []
        for t in range(n):
            w = wide[m + t, pl.ds(begin, FX), :]
            new += [u_ref[y + 2 * t] + w, u_ref[y + 2 * t + 1] + w]
        for t in range(2 * n):
            dst[y + t] = new[t]

    rows(lo, hi, add)


def middle_kernel(scal, src, fbx, fby, fbz, fdiag, finv, u2, here, near, swapped,
                  mbx, mby, mbz, mdiag, minv, lbx, lby, lbz, linv, u2_out, pack,
                  joined, rhs, absorb, conduct, m1, m2, lrhs, l1, l2, labsorb, lconduct, tmp, wide, fa, fb):
    fine = Level(fbx, fby, fbz, fdiag, finv, 1, False)
    mid = Level(mbx, mby, mbz, mdiag, minv, 2, True)
    low = Level(lbx, lby, lbz, None, linv, 4, True)
    gather_rows(scal, here, near, swapped, joined, 3)
    unpack_rows(joined, 0, rhs)
    unpack_rows(joined, 2, absorb)
    unpack_rows(joined, 4, conduct)
    mid.build(conduct, absorb, 2, 38, 4.0)
    restrict_low(lambda y, n: [absorb[y + t] for t in range(n)], tmp, labsorb, 1, 19)
    restrict_low(lambda y, n: [conduct[y + t] for t in range(n)], tmp, lconduct, 1, 19)
    low.build(lconduct, labsorb, 2, 18, 16.0)
    coarse(mid, low, rhs, m1, m2, lrhs, l1, l2, tmp, 0)
    prolong_add(scal, m2, wide, u2, fa, 12, 28)
    fine.sweep(fb, fa, src, 3, ROWS - 3)
    fine.sweep(fa, fb, src, 4, ROWS - 4)
    fine.sweep(fb, fa, src, 5, ROWS - 5)
    zero = jnp.zeros((FX, 128), F32)
    for y in (*range(6), *range(ROWS - 6, ROWS)):
        u2_out[y] = zero
    fine.sweep(u2_out, fb, src, 6, ROWS - 6)
    tiles = restrict_own([r[8:16] for r in fine.residual(u2_out, src, HALO, 16)])
    for i, t in enumerate(tiles):
        pack[i] = t


def last_kernel(scal, src, fbx, fby, fbz, fdiag, finv, u2, here, near, swapped,
                mbx, mby, mbz, mdiag, minv, lbx, lby, lbz, linv,
                out, out_res,
                joined, rhs, m1, m2, lrhs, l1, l2, tmp, wide, fa, fb):
    fine = Level(fbx, fby, fbz, fdiag, finv, 1, False)
    mid = Level(mbx, mby, mbz, mdiag, minv, 2, True)
    low = Level(lbx, lby, lbz, None, linv, 4, True)
    gather_rows(scal, here, near, swapped, joined, 1)
    unpack_rows(joined, 0, rhs)
    coarse(mid, low, rhs, m1, m2, lrhs, l1, l2, tmp, 1)
    prolong_add(scal, m2, wide, u2, fa, 14, 26)
    fine.sweep(fb, fa, src, 7, ROWS - 7)
    fine.sweep(fa, fb, src, 8, ROWS - 8)

    def finish(y, n):
        r = fine.residual(fa, src, HALO + y, n)
        for t in range(n):
            at = pl.ds(y + t, 8, stride=16)
            out[at, :] = fa[HALO + y + t, 8:16, :]
            out_res[at, :] = r[t][8:16]

    rows(0, 16, finish)


def call(kernel, outs, scratch, *args):
    return pl.pallas_call(
        kernel,
        out_shape=[jax.ShapeDtypeStruct(s, F32) for s in outs],
        in_specs=[pl.BlockSpec(memory_space=pltpu.SMEM)]
        + [pl.BlockSpec(memory_space=pltpu.VMEM)] * (len(args) - 1),
        out_specs=[pl.BlockSpec(memory_space=pltpu.VMEM)] * len(outs),
        scratch_shapes=[pltpu.VMEM(s, F32) for s in scratch],
        compiler_params=pltpu.CompilerParams(vmem_limit_bytes=VMEM_LIMIT),
    )(*args)


def other_core(array):
    return lax.ppermute(array, "dev", [(i, i ^ 1) for i in range(8)])


def one_away(g, core):
    return 1 if g % 2 == core else -1


def two_away(g, core):
    return 2 if g // 2 % 2 != core else -2


def spread(pack, ends=None):
    peers, devs = lax.axis_size("grp"), lax.axis_size("dev")

    def from_beside(array, by):
        pairs = []
        for g in range(peers):
            for d in range(devs):
                there = g + by(g, d % 2)
                if 0 <= there < peers:
                    pairs.append((there * devs + d, g * devs + d))
        return lax.ppermute(array, ("grp", "dev"), pairs)

    here = jnp.broadcast_to(pack, (devs,) + pack.shape)
    if ends is not None:
        d = lax.axis_index("dev")
        mine = jnp.where(jnp.arange(devs)[:, None, None] < d, ends[0], ends[1])
        here = jnp.concatenate([here, mine.reshape(devs, 2, 8, 128)], axis=1)
    here = lax.all_to_all(here, "dev", 0, 0)
    if ends is not None:
        ends = here[:, -2:].reshape(devs, 16, 128)
        here = here[:, :-2]
    near = jnp.stack([from_beside(here, one_away), from_beside(here, two_away)])
    return ends, here, near, other_core(near)


def local(source, absorb, conduct):
    peers = lax.axis_size("grp")
    d = lax.axis_index("dev")
    g, core = lax.axis_index("grp"), d % 2
    scal = jnp.stack([core, d, g % 2 == core, g // 2 % 2 != core]).astype(jnp.int32)

    fine = jnp.stack([source, absorb, conduct]).transpose(0, 2, 1, 3)
    even = g % 2 == 0
    first, last = fine[:, :HALO], fine[:, 16 - HALO:]

    def swap_rows(array, low):
        pairs = [(i, i + 1) for i in range(low, peers - 1, 2)]
        return lax.ppermute(array, "grp", pairs + [(j, i) for i, j in pairs])

    one = swap_rows(jnp.where(even, last, first), 0)
    two = swap_rows(jnp.where(even, first, last), 1)
    before, after = jnp.where(even, two, one), jnp.where(even, one, two)
    fine = jnp.concatenate([before, fine, after], axis=1)

    def other_chip(array):
        return lax.ppermute(array, "dev", [(1, 2), (2, 1), (3, 4), (4, 3), (5, 6), (6, 5)])

    one, two = fine[:, HALO - 3:ROWS - HALO + 3:2], fine[:, HALO - 2:ROWS - HALO + 3:2]
    near = [jnp.concatenate([one[:, :, x:x + 4], two[:, :, x:x + 4]], axis=2) for x in (0, 4)]
    near_a = other_core(jnp.where(core == 0, near[1], near[0]))
    near_b = other_chip(jnp.where(core == 0, near[0], near[1]))
    via_a, via_b = other_core(fine), other_chip(fine)
    block, wide_mid, wide_low = (ROWS, FX, 128), (MROWS, MX, 128), (LROWS, LX, 128)
    pack, ends = call(first_kernel, [(6, 8, 128), (2, 16, 128)], [block] * 10, scal, fine, near_a, near_b)
    ends, *parts = spread(pack, ends)
    *state, u2 = call(rim_kernel, [block] * 7, [block] * 3, scal, fine, via_a, via_b, ends)
    *coefs, u2, pack = call(
        middle_kernel,
        [wide_mid] * 5 + [wide_low] * 4 + [block, (2, 8, 128)],
        [(5, 6, 64, 128)] + [wide_mid] * 5 + [wide_low] * 5 + [(20, MX, 128), (MROWS, 80, 128), block, block],
        scal, *state, u2, *parts,
    )
    _, *parts = spread(pack)
    out, res = call(
        last_kernel,
        [(128, 128), (128, 128)],
        [(5, 2, 64, 128)] + [wide_mid] * 3 + [wide_low] * 3 + [(20, MX, 128), (MROWS, 80, 128), block, block],
        scal, *state, u2, *parts, *coefs,
    )
    return out.reshape(8, 16, 128), res.reshape(8, 16, 128)


def solution(mesh):
    spec = P("dev", "grp", None)
    return jax.shard_map(local, mesh=mesh, in_specs=(spec,) * 3, out_specs=(spec,) * 2, check_vma=False)
```

```python
import functools

import jax
import jax.numpy as jnp
from jax import lax
from jax.experimental import pallas as pl
from jax.experimental.pallas import tpu as pltpu
from jax.sharding import PartitionSpec as P

RELAX = 0.8
HALO = 9
ROWS = 16 + 2 * HALO
FX = 24
MROWS = 40
MX = 16
LROWS = 20
LX = 8
VMEM_LIMIT = 40 * 1024 * 1024

F32 = jnp.float32


def rows(lo, hi, body):
    body(lo, hi - lo)


def lanes(shape):
    return lax.broadcasted_iota(jnp.int32, shape, 1)


def planes(shape):
    return lax.broadcasted_iota(jnp.int32, shape, 0)


def up(value, axis, by):
    return pltpu.roll(value, value.shape[axis] - by, axis)


def down(value, axis, by):
    return pltpu.roll(value, by, axis)


def next_plane(value):
    value = up(value, 0, 1)
    last = value[-8:]
    last = jnp.where(planes((8, 128)) == 7, up(last, 1, 1), last)
    return last if value.shape[0] == 8 else jnp.concatenate([value[:-8], last])


def previous_plane(value):
    value = down(value, 0, 1)
    first = value[:8]
    first = jnp.where(planes((8, 128)) == 0, down(first, 1, 1), first)
    return first if value.shape[0] == 8 else jnp.concatenate([first, value[8:]])


class Level:
    def __init__(self, bx, by, bz, diag, inv, width, folded):
        self.bx, self.by, self.bz, self.diag, self.inv, self.width = bx, by, bz, diag, inv, width
        self.folded = folded
        self.next = next_plane if folded else lambda value: up(value, 0, 1)
        self.previous = previous_plane if folded else lambda value: down(value, 0, 1)

    def beside(self, u_ref, y, n):
        u = [u_ref[y - 1 + t] for t in range(n + 2)]
        by = [self.by[y - 1 + t] for t in range(n + 1)]
        flow = [by[t] * u[t + 1] for t in range(n + 1)]
        acc = []
        for t in range(n):
            here, bx, bz = u[t + 1], self.bx[y + t], self.bz[y + t]
            x = bx * self.next(here) + self.previous(bx * here)
            z = bz * up(here, 1, self.width) + down(bz * here, 1, self.width)
            acc.append((by[t] * u[t] + by[t + 1] * u[t + 2]) + (x + z))
        return u[1:-1], acc

    def sweep(self, dst, src, rhs, lo, hi):
        def body(y, n):
            u, acc = self.beside(src, y, n)
            new = [(1.0 - RELAX) * u[t] + self.inv[y + t] * (rhs[y + t] + acc[t]) for t in range(n)]
            for t in range(n):
                dst[y + t] = new[t]

        rows(lo, hi, body)

    def residual(self, u_ref, rhs, y, n):
        u, acc = self.beside(u_ref, y, n)
        return [rhs[y + t] - self.diag[y + t] * u[t] + acc[t] for t in range(n)]

    def build(self, conduct, absorb, lo, hi, spacing):
        shape = conduct.shape[1:]
        z, x = lanes(shape), planes(shape)
        half = 0.5 / spacing
        final = jnp.logical_and(x == shape[0] - 1, z % 2 == 1)
        initial = jnp.logical_and(x == 0, z % 2 == 0)

        def body(y, n):
            c = [conduct[y - 1 + t] for t in range(n + 2)]
            done = []
            for t in range(n):
                here = c[t + 1]
                xp, xm = self.next(here), self.previous(here)
                if self.folded:
                    xp = jnp.where(final, 0.0, xp)
                    xm = jnp.where(initial, 0.0, xm)
                zp = jnp.where(z >= shape[1] - self.width, 0.0, up(here, 1, self.width))
                zm = jnp.where(z < self.width, 0.0, down(here, 1, self.width))
                bx = (here + xp) * half
                if self.folded:
                    bx = jnp.where(final, 0.0, bx)
                by = (here + c[t + 2]) * half
                bz = jnp.where(z >= shape[1] - self.width, 0.0, (here + zp) * half)
                a = absorb[y + t]
                diag = a + (3.0 / spacing) * here + half * (((xp + xm) + (c[t] + c[t + 2])) + (zp + zm))
                done.append((bx, by, bz, diag, jnp.where(a > 0.0, RELAX / diag, 0.0)))
            for t in range(n):
                for ref, value in zip((self.bx, self.by, self.bz, self.diag, self.inv), done[t]):
                    if ref is not None:
                        ref[y + t] = value

        self.by[lo - 1] = (conduct[lo - 1] + conduct[lo]) * half
        rows(lo, hi, body)


def pair_lanes(t, width):
    first = (lanes(t.shape) // width) % 2 == 0
    return t + jnp.where(first, up(t, 1, width), down(t, 1, width))


def pair_planes(t):
    first = planes(t.shape) % 2 == 0
    return t + jnp.where(first, up(t, 0, 1), down(t, 0, 1))


def pack_rows(row_of):
    x, z = planes((8, 128)) % 2, lanes((8, 128)) % 2
    tiles = []
    for k in range(2):
        r = [row_of(4 * k + t) for t in range(4)]
        tiles.append(jnp.where(x == 0, jnp.where(z == 0, r[0], r[1]), jnp.where(z == 0, r[2], r[3])))
    return tiles


def restrict_own(r):
    def row_of(j):
        return pair_planes(pair_lanes(r[2 * j] + r[2 * j + 1], 1)) * 0.125

    return pack_rows(row_of)


def restrict_low(fine_rows, tmp, dst, lo, hi):
    def body(i, n):
        r = fine_rows(2 * i, 2 * n)
        for t in range(n):
            tmp[t] = r[2 * t] + r[2 * t + 1]
        for t in range(n):
            pair = tmp[t, pl.ds(0, LX, stride=2), :] + tmp[t, pl.ds(1, LX, stride=2), :]
            dst[i + t] = pair_lanes(pair, 2) * 0.125

    rows(lo, hi, body)


def scale(dst, factor, src, lo, hi):
    def body(y, n):
        new = [factor[y + t] * src[y + t] for t in range(n)]
        for t in range(n):
            dst[y + t] = new[t]

    rows(lo, hi, body)


def join_planes(scal, own, via_a, via_b, arr, dst, lo, hi):
    even = scal[0] == 0
    for y in range(lo, hi):
        a, b = via_a[arr * ROWS + y], via_b[arr * ROWS + y]
        dst[y, 0:8, :] = jnp.where(even, b, a)
        dst[y, 8:16, :] = own[arr, y]
        dst[y, 16:24, :] = jnp.where(even, a, b)


def first_kernel(scal, own, near_a, near_b, pack, ends,
                 src, absorb, conduct, bx, by, bz, diag, inv, u1, u2):
    even = scal[0] == 0
    for arr, dst in ((0, src), (1, absorb), (2, conduct)):
        for i in range(22):
            y = HALO - 3 + i
            a, b = near_a[arr, i // 2], near_b[arr, i // 2]
            left, right = jnp.where(even, b, a), jnp.where(even, a, b)
            dst[y, 0:8, :] = down(left, 0, 4) if i % 2 == 0 else left
            dst[y, 8:16, :] = own[arr, y]
            dst[y, 16:24, :] = right if i % 2 == 0 else down(right, 0, 4)
    level = Level(bx, by, bz, diag, inv, 1, False)
    level.build(conduct, absorb, HALO - 2, ROWS - HALO + 2, 1.0)
    scale(u1, inv, src, HALO - 2, ROWS - HALO + 2)
    for y in range(16):
        for i, x in enumerate((8, 15)):
            ends[i, y:y + 1, :] = u1[HALO + y, x:x + 1, :]
    level.sweep(u2, u1, src, HALO - 1, ROWS - HALO + 1)
    tiles = restrict_own([r[8:16] for r in level.residual(u2, src, HALO, 16)])
    tiles += restrict_own([absorb[HALO + i, 8:16, :] for i in range(16)])
    tiles += restrict_own([conduct[HALO + i, 8:16, :] for i in range(16)])
    for i, t in enumerate(tiles):
        pack[i] = t


def rim_kernel(scal, own, via_a, via_b,
               src, bx, by, bz, diag, inv, u2,
               absorb, conduct, u1):
    for arr, dst in ((0, src), (1, absorb), (2, conduct)):
        join_planes(scal, own, via_a, via_b, arr, dst, 0, ROWS)
    level = Level(bx, by, bz, diag, inv, 1, False)
    level.build(conduct, absorb, 1, ROWS - 1, 1.0)
    x = planes((FX, 128))
    even = scal[0] == 0
    for y in range(1, ROWS - 1):
        u = inv[y] * src[y]
        if 0 <= y - HALO < 16:
            i, at = divmod(y - HALO, 8)
            a, b = (via[3 * ROWS + i, at:at + 1, :] for via in (via_a, via_b))
            left, right = jnp.where(even, b, a), jnp.where(even, a, b)
            u = jnp.where(x == 0, left, jnp.where(x == FX - 1, right, u))
        u1[y] = u
    zero = jnp.zeros((FX, 128), F32)
    for y in (0, 1, ROWS - 2, ROWS - 1):
        u2[y] = zero
    level.sweep(u2, u1, src, 2, ROWS - 2)


def gather_rows(scal, here, near, swapped, joined, arrays):
    def copy(j, source):
        for t in range(2 * arrays):
            for dev in range(8):
                joined[j, t, 8 * dev:8 * dev + 8, :] = source[dev, t]

    copy(2, here)
    for i in range(2):
        after, before = 3 + i, 1 - i
        near_after = scal[2 + i] != 0

        @pl.when(near_after)
        def _():
            copy(after, near.at[i])
            copy(before, swapped.at[i])

        @pl.when(jnp.logical_not(near_after))
        def _():
            copy(after, swapped.at[i])
            copy(before, near.at[i])


def unpack_rows(joined, tile, dst):
    z = lanes((MX, 128)) % 2 == 0

    for j in range(5):
        for k in range(2):
            for a in range(2):
                v = joined[j, tile + k, pl.ds(a, 2 * MX, stride=2), :]
                v, w = v[:MX], v[MX:]
                y = j * 8 + 4 * k + 2 * a
                dst[y] = jnp.where(z, v, down(w, 1, 1))
                dst[y + 1] = jnp.where(z, up(v, 1, 1), w)


def coarse(mid, low, rhs, m1, m2, lrhs, l1, l2, tmp, k):
    scale(m1, mid.inv, rhs, 2 + 2 * k, 38 - 2 * k)
    mid.sweep(m2, m1, rhs, 3 + 2 * k, 37 - 2 * k)
    restrict_low(functools.partial(mid.residual, m2, rhs), tmp, lrhs, 2 + k, 18 - k)
    scale(l1, low.inv, lrhs, 2 + k, 18 - k)
    low.sweep(l2, l1, lrhs, 3 + k, 17 - k)
    low.sweep(l1, l2, lrhs, 4 + k, 16 - k)
    low.sweep(l2, l1, lrhs, 5 + k, 15 - k)

    for i in range(5 + k, 15 - k):
        v = l2[i]
        for y in (2 * i, 2 * i + 1):
            for a in range(2):
                at = pl.ds(a, LX, stride=2)
                m2[y, at, :] = m2[y, at, :] + v

    mid.sweep(m1, m2, rhs, 11 + 2 * k, 29 - 2 * k)
    mid.sweep(m2, m1, rhs, 12 + 2 * k, 28 - 2 * k)


def prolong_add(scal, m2, wide, u_ref, dst, lo, hi):
    begin = pl.multiple_of(scal[1] * 8, 8)
    zero = jnp.zeros((8, 128), F32)
    z = lanes((MX, 128)) % 2 == 0

    def body(m, n):
        for t in range(n):
            v = m2[m + t]
            low, high = jnp.where(z, v, down(v, 1, 1)), jnp.where(z, up(v, 1, 1), v)
            wide[m + t, 0:8, :] = zero
            wide[m + t, 72:80, :] = zero
            for a in range(2):
                wide[m + t, pl.ds(8 + a, MX, stride=2), :] = low
                wide[m + t, pl.ds(40 + a, MX, stride=2), :] = high

    rows(lo, hi, body)

    def add(m, n):
        y = 2 * m - 32 + HALO
        new = []
        for t in range(n):
            w = wide[m + t, pl.ds(begin, FX), :]
            new += [u_ref[y + 2 * t] + w, u_ref[y + 2 * t + 1] + w]
        for t in range(2 * n):
            dst[y + t] = new[t]

    rows(lo, hi, add)


def middle_kernel(scal, src, fbx, fby, fbz, fdiag, finv, u2, here, near, swapped,
                  mbx, mby, mbz, mdiag, minv, lbx, lby, lbz, linv, u2_out, pack,
                  joined, rhs, absorb, conduct, m1, m2, lrhs, l1, l2, labsorb, lconduct, tmp, wide, fa, fb):
    fine = Level(fbx, fby, fbz, fdiag, finv, 1, False)
    mid = Level(mbx, mby, mbz, mdiag, minv, 2, True)
    low = Level(lbx, lby, lbz, None, linv, 4, True)
    gather_rows(scal, here, near, swapped, joined, 3)
    unpack_rows(joined, 0, rhs)
    unpack_rows(joined, 2, absorb)
    unpack_rows(joined, 4, conduct)
    mid.build(conduct, absorb, 2, 38, 4.0)
    restrict_low(lambda y, n: [absorb[y + t] for t in range(n)], tmp, labsorb, 1, 19)
    restrict_low(lambda y, n: [conduct[y + t] for t in range(n)], tmp, lconduct, 1, 19)
    low.build(lconduct, labsorb, 2, 18, 16.0)
    coarse(mid, low, rhs, m1, m2, lrhs, l1, l2, tmp, 0)
    prolong_add(scal, m2, wide, u2, fa, 12, 28)
    fine.sweep(fb, fa, src, 3, ROWS - 3)
    fine.sweep(fa, fb, src, 4, ROWS - 4)
    fine.sweep(fb, fa, src, 5, ROWS - 5)
    zero = jnp.zeros((FX, 128), F32)
    for y in (*range(6), *range(ROWS - 6, ROWS)):
        u2_out[y] = zero
    fine.sweep(u2_out, fb, src, 6, ROWS - 6)
    tiles = restrict_own([r[8:16] for r in fine.residual(u2_out, src, HALO, 16)])
    for i, t in enumerate(tiles):
        pack[i] = t


def last_kernel(scal, src, fbx, fby, fbz, fdiag, finv, u2, here, near, swapped,
                mbx, mby, mbz, mdiag, minv, lbx, lby, lbz, linv,
                out, out_res,
                joined, rhs, m1, m2, lrhs, l1, l2, tmp, wide, fa, fb):
    fine = Level(fbx, fby, fbz, fdiag, finv, 1, False)
    mid = Level(mbx, mby, mbz, mdiag, minv, 2, True)
    low = Level(lbx, lby, lbz, None, linv, 4, True)
    gather_rows(scal, here, near, swapped, joined, 1)
    unpack_rows(joined, 0, rhs)
    coarse(mid, low, rhs, m1, m2, lrhs, l1, l2, tmp, 1)
    prolong_add(scal, m2, wide, u2, fa, 14, 26)
    fine.sweep(fb, fa, src, 7, ROWS - 7)
    fine.sweep(fa, fb, src, 8, ROWS - 8)

    def finish(y, n):
        r = fine.residual(fa, src, HALO + y, n)
        for t in range(n):
            at = pl.ds(y + t, 8, stride=16)
            out[at, :] = fa[HALO + y + t, 8:16, :]
            out_res[at, :] = r[t][8:16]

    rows(0, 16, finish)


def call(kernel, outs, scratch, *args):
    return pl.pallas_call(
        kernel,
        out_shape=[jax.ShapeDtypeStruct(s, F32) for s in outs],
        in_specs=[pl.BlockSpec(memory_space=pltpu.SMEM)]
        + [pl.BlockSpec(memory_space=pltpu.VMEM)] * (len(args) - 1),
        out_specs=[pl.BlockSpec(memory_space=pltpu.VMEM)] * len(outs),
        scratch_shapes=[pltpu.VMEM(s, F32) for s in scratch],
        compiler_params=pltpu.CompilerParams(vmem_limit_bytes=VMEM_LIMIT),
    )(*args)


def other_core(array):
    return lax.ppermute(array, "dev", [(i, i ^ 1) for i in range(8)])


def one_away(g, core):
    return 1 if g % 2 == core else -1


def two_away(g, core):
    return 2 if g // 2 % 2 != core else -2


def spread(pack):
    peers, devs = lax.axis_size("grp"), lax.axis_size("dev")

    def from_beside(array, by):
        pairs = []
        for g in range(peers):
            for d in range(devs):
                there = g + by(g, d % 2)
                if 0 <= there < peers:
                    pairs.append((there * devs + d, g * devs + d))
        return lax.ppermute(array, ("grp", "dev"), pairs)

    here = lax.all_to_all(jnp.broadcast_to(pack, (devs,) + pack.shape), "dev", 0, 0)
    near = jnp.stack([from_beside(here, one_away), from_beside(here, two_away)])
    return here, near, other_core(near)


def local(source, absorb, conduct):
    peers = lax.axis_size("grp")
    d = lax.axis_index("dev")
    g, core = lax.axis_index("grp"), d % 2
    scal = jnp.stack([core, d, g % 2 == core, g // 2 % 2 != core]).astype(jnp.int32)

    fine = jnp.stack([source, absorb, conduct]).transpose(0, 2, 1, 3)
    even = g % 2 == 0
    first, last = fine[:, :HALO], fine[:, 16 - HALO:]

    def swap_rows(array, low):
        pairs = [(i, i + 1) for i in range(low, peers - 1, 2)]
        return lax.ppermute(array, "grp", pairs + [(j, i) for i, j in pairs])

    one = swap_rows(jnp.where(even, last, first), 0)
    two = swap_rows(jnp.where(even, first, last), 1)
    before, after = jnp.where(even, two, one), jnp.where(even, one, two)
    fine = jnp.concatenate([before, fine, after], axis=1)

    def other_chip(array):
        return lax.ppermute(array, "dev", [(1, 2), (2, 1), (3, 4), (4, 3), (5, 6), (6, 5)])

    one, two = fine[:, HALO - 3:ROWS - HALO + 3:2], fine[:, HALO - 2:ROWS - HALO + 3:2]
    near = [jnp.concatenate([one[:, :, x:x + 4], two[:, :, x:x + 4]], axis=2) for x in (0, 4)]
    near_a = other_core(jnp.where(core == 0, near[1], near[0]))
    near_b = other_chip(jnp.where(core == 0, near[0], near[1]))
    block, wide_mid, wide_low = (ROWS, FX, 128), (MROWS, MX, 128), (LROWS, LX, 128)
    pack, ends = call(first_kernel, [(6, 8, 128), (2, 16, 128)], [block] * 10, scal, fine, near_a, near_b)
    parts = spread(pack)
    whole, ends = fine.reshape(3 * ROWS, 8, 128), ends.reshape(2, 2, 8, 128)
    via_a = other_core(jnp.concatenate([whole, jnp.where(core == 0, ends[0], ends[1])]))
    via_b = other_chip(jnp.concatenate([whole, jnp.where(core == 0, ends[1], ends[0])]))
    *state, u2 = call(rim_kernel, [block] * 7, [block] * 3, scal, fine, via_a, via_b)
    *coefs, u2, pack = call(
        middle_kernel,
        [wide_mid] * 5 + [wide_low] * 4 + [block, (2, 8, 128)],
        [(5, 6, 64, 128)] + [wide_mid] * 5 + [wide_low] * 5 + [(20, MX, 128), (MROWS, 80, 128), block, block],
        scal, *state, u2, *parts,
    )
    parts = spread(pack)
    out, res = call(
        last_kernel,
        [(128, 128), (128, 128)],
        [(5, 2, 64, 128)] + [wide_mid] * 3 + [wide_low] * 3 + [(20, MX, 128), (MROWS, 80, 128), block, block],
        scal, *state, u2, *parts, *coefs,
    )
    return out.reshape(8, 16, 128), res.reshape(8, 16, 128)


def solution(mesh):
    spec = P("dev", "grp", None)
    return jax.shard_map(local, mesh=mesh, in_specs=(spec,) * 3, out_specs=(spec,) * 2, check_vma=False)
```

```python
import functools

import jax
import jax.numpy as jnp
from jax import lax
from jax.experimental import pallas as pl
from jax.experimental.pallas import tpu as pltpu
from jax.sharding import PartitionSpec as P

RELAX = 0.8
HALO = 9
ROWS = 16 + 2 * HALO
FX = 24
MROWS = 40
MX = 16
LROWS = 20
LX = 8
VMEM_LIMIT = 40 * 1024 * 1024

F32 = jnp.float32


def rows(lo, hi, body):
    body(lo, hi - lo)


def lanes(shape):
    return lax.broadcasted_iota(jnp.int32, shape, 1)


def planes(shape):
    return lax.broadcasted_iota(jnp.int32, shape, 0)


def up(value, axis, by):
    return pltpu.roll(value, value.shape[axis] - by, axis)


def down(value, axis, by):
    return pltpu.roll(value, by, axis)


def next_plane(value):
    value = up(value, 0, 1)
    last = value[-8:]
    last = jnp.where(planes((8, 128)) == 7, up(last, 1, 1), last)
    return last if value.shape[0] == 8 else jnp.concatenate([value[:-8], last])


def previous_plane(value):
    value = down(value, 0, 1)
    first = value[:8]
    first = jnp.where(planes((8, 128)) == 0, down(first, 1, 1), first)
    return first if value.shape[0] == 8 else jnp.concatenate([first, value[8:]])


class Level:
    def __init__(self, bx, by, bz, diag, inv, width, folded):
        self.bx, self.by, self.bz, self.diag, self.inv, self.width = bx, by, bz, diag, inv, width
        self.folded = folded
        self.next = next_plane if folded else lambda value: up(value, 0, 1)
        self.previous = previous_plane if folded else lambda value: down(value, 0, 1)

    def beside(self, u_ref, y, n):
        u = [u_ref[y - 1 + t] for t in range(n + 2)]
        by = [self.by[y - 1 + t] for t in range(n + 1)]
        flow = [by[t] * u[t + 1] for t in range(n + 1)]
        acc = []
        for t in range(n):
            here, bx, bz = u[t + 1], self.bx[y + t], self.bz[y + t]
            x = bx * self.next(here) + self.previous(bx * here)
            z = bz * up(here, 1, self.width) + down(bz * here, 1, self.width)
            acc.append((by[t] * u[t] + by[t + 1] * u[t + 2]) + (x + z))
        return u[1:-1], acc

    def sweep(self, dst, src, rhs, lo, hi):
        def body(y, n):
            u, acc = self.beside(src, y, n)
            new = [(1.0 - RELAX) * u[t] + self.inv[y + t] * (rhs[y + t] + acc[t]) for t in range(n)]
            for t in range(n):
                dst[y + t] = new[t]

        rows(lo, hi, body)

    def residual(self, u_ref, rhs, y, n):
        u, acc = self.beside(u_ref, y, n)
        return [rhs[y + t] - self.diag[y + t] * u[t] + acc[t] for t in range(n)]

    def build(self, conduct, absorb, lo, hi, spacing):
        shape = conduct.shape[1:]
        z, x = lanes(shape), planes(shape)
        half = 0.5 / spacing
        final = jnp.logical_and(x == shape[0] - 1, z % 2 == 1)
        initial = jnp.logical_and(x == 0, z % 2 == 0)

        def body(y, n):
            c = [conduct[y - 1 + t] for t in range(n + 2)]
            done = []
            for t in range(n):
                here = c[t + 1]
                xp, xm = self.next(here), self.previous(here)
                if self.folded:
                    xp = jnp.where(final, 0.0, xp)
                    xm = jnp.where(initial, 0.0, xm)
                zp = jnp.where(z >= shape[1] - self.width, 0.0, up(here, 1, self.width))
                zm = jnp.where(z < self.width, 0.0, down(here, 1, self.width))
                bx = (here + xp) * half
                if self.folded:
                    bx = jnp.where(final, 0.0, bx)
                by = (here + c[t + 2]) * half
                bz = jnp.where(z >= shape[1] - self.width, 0.0, (here + zp) * half)
                a = absorb[y + t]
                diag = a + (3.0 / spacing) * here + half * (((xp + xm) + (c[t] + c[t + 2])) + (zp + zm))
                done.append((bx, by, bz, diag, jnp.where(a > 0.0, RELAX / diag, 0.0)))
            for t in range(n):
                for ref, value in zip((self.bx, self.by, self.bz, self.diag, self.inv), done[t]):
                    if ref is not None:
                        ref[y + t] = value

        self.by[lo - 1] = (conduct[lo - 1] + conduct[lo]) * half
        rows(lo, hi, body)


def pair_lanes(t, width):
    first = (lanes(t.shape) // width) % 2 == 0
    return t + jnp.where(first, up(t, 1, width), down(t, 1, width))


def pair_planes(t):
    first = planes(t.shape) % 2 == 0
    return t + jnp.where(first, up(t, 0, 1), down(t, 0, 1))


def pack_rows(row_of):
    x, z = planes((8, 128)) % 2, lanes((8, 128)) % 2
    tiles = []
    for k in range(2):
        r = [row_of(4 * k + t) for t in range(4)]
        tiles.append(jnp.where(x == 0, jnp.where(z == 0, r[0], r[1]), jnp.where(z == 0, r[2], r[3])))
    return tiles


def restrict_own(r):
    def row_of(j):
        return pair_planes(pair_lanes(r[2 * j] + r[2 * j + 1], 1)) * 0.125

    return pack_rows(row_of)


def restrict_low(fine_rows, tmp, dst, lo, hi):
    def body(i, n):
        r = fine_rows(2 * i, 2 * n)
        for t in range(n):
            tmp[t] = r[2 * t] + r[2 * t + 1]
        for t in range(n):
            pair = tmp[t, pl.ds(0, LX, stride=2), :] + tmp[t, pl.ds(1, LX, stride=2), :]
            dst[i + t] = pair_lanes(pair, 2) * 0.125

    rows(lo, hi, body)


class FirstSweep:
    def __init__(self, level, rhs):
        self.level, self.rhs = level, rhs

    def __getitem__(self, y):
        return self.level.inv[y] * self.rhs[y]


def join_planes(scal, own, via_a, via_b, arr, dst, lo, hi):
    even = scal[0] == 0
    for y in range(lo, hi):
        a, b = via_a[arr * ROWS + y], via_b[arr * ROWS + y]
        dst[y, 0:8, :] = jnp.where(even, b, a)
        dst[y, 8:16, :] = own[arr, y]
        dst[y, 16:24, :] = jnp.where(even, a, b)


def first_kernel(scal, own, near_a, near_b, pack, ends,
                 src, absorb, conduct, bx, by, bz, diag, inv, u2):
    even = scal[0] == 0
    for arr, dst in ((0, src), (1, absorb), (2, conduct)):
        for i in range(22):
            y = HALO - 3 + i
            a, b = near_a[arr, i // 2], near_b[arr, i // 2]
            left, right = jnp.where(even, b, a), jnp.where(even, a, b)
            dst[y, 0:8, :] = down(left, 0, 4) if i % 2 == 0 else left
            dst[y, 8:16, :] = own[arr, y]
            dst[y, 16:24, :] = right if i % 2 == 0 else down(right, 0, 4)
    level = Level(bx, by, bz, diag, inv, 1, False)
    level.build(conduct, absorb, HALO - 2, ROWS - HALO + 2, 1.0)
    u1 = FirstSweep(level, src)
    for y in range(16):
        own_rows = inv[HALO + y, 8:16, :] * src[HALO + y, 8:16, :]
        ends[0, y:y + 1, :] = own_rows[0:1]
        ends[1, y:y + 1, :] = own_rows[7:8]
    level.sweep(u2, u1, src, HALO - 1, ROWS - HALO + 1)
    tiles = restrict_own([r[8:16] for r in level.residual(u2, src, HALO, 16)])
    tiles += restrict_own([absorb[HALO + i, 8:16, :] for i in range(16)])
    tiles += restrict_own([conduct[HALO + i, 8:16, :] for i in range(16)])
    for i, t in enumerate(tiles):
        pack[i] = t


def rim_kernel(scal, own, via_a, via_b,
               src, bx, by, bz, diag, inv, u2,
               absorb, conduct, u1):
    for arr, dst in ((0, src), (1, absorb), (2, conduct)):
        join_planes(scal, own, via_a, via_b, arr, dst, 0, ROWS)
    level = Level(bx, by, bz, diag, inv, 1, False)
    level.build(conduct, absorb, 1, ROWS - 1, 1.0)
    x = planes((FX, 128))
    even = scal[0] == 0
    for y in range(1, ROWS - 1):
        u = inv[y] * src[y]
        if 0 <= y - HALO < 16:
            i, at = divmod(y - HALO, 8)
            a, b = (via[3 * ROWS + i, at:at + 1, :] for via in (via_a, via_b))
            left, right = jnp.where(even, b, a), jnp.where(even, a, b)
            u = jnp.where(x == 0, left, jnp.where(x == FX - 1, right, u))
        u1[y] = u
    zero = jnp.zeros((FX, 128), F32)
    for y in (0, 1, ROWS - 2, ROWS - 1):
        u2[y] = zero
    level.sweep(u2, u1, src, 2, ROWS - 2)


def gather_rows(scal, here, near, swapped, joined, arrays):
    def copy(j, source):
        for t in range(2 * arrays):
            for dev in range(8):
                joined[j, t, 8 * dev:8 * dev + 8, :] = source[dev, t]

    copy(2, here)
    for i in range(2):
        after, before = 3 + i, 1 - i
        near_after = scal[2 + i] != 0

        @pl.when(near_after)
        def _():
            copy(after, near.at[i])
            copy(before, swapped.at[i])

        @pl.when(jnp.logical_not(near_after))
        def _():
            copy(after, swapped.at[i])
            copy(before, near.at[i])


def unpack_rows(joined, tile, dst):
    z = lanes((MX, 128)) % 2 == 0

    for j in range(5):
        for k in range(2):
            for a in range(2):
                v = joined[j, tile + k, pl.ds(a, 2 * MX, stride=2), :]
                v, w = v[:MX], v[MX:]
                y = j * 8 + 4 * k + 2 * a
                dst[y] = jnp.where(z, v, down(w, 1, 1))
                dst[y + 1] = jnp.where(z, up(v, 1, 1), w)


def coarse(mid, low, rhs, m1, m2, lrhs, l1, l2, tmp, k):
    mid.sweep(m2, FirstSweep(mid, rhs), rhs, 3 + 2 * k, 37 - 2 * k)
    restrict_low(functools.partial(mid.residual, m2, rhs), tmp, lrhs, 2 + k, 18 - k)
    low.sweep(l2, FirstSweep(low, lrhs), lrhs, 3 + k, 17 - k)
    low.sweep(l1, l2, lrhs, 4 + k, 16 - k)
    low.sweep(l2, l1, lrhs, 5 + k, 15 - k)

    for i in range(5 + k, 15 - k):
        v = l2[i]
        for y in (2 * i, 2 * i + 1):
            for a in range(2):
                at = pl.ds(a, LX, stride=2)
                m2[y, at, :] = m2[y, at, :] + v

    mid.sweep(m1, m2, rhs, 11 + 2 * k, 29 - 2 * k)
    mid.sweep(m2, m1, rhs, 12 + 2 * k, 28 - 2 * k)


def prolong_add(scal, m2, wide, u_ref, dst, lo, hi):
    begin = pl.multiple_of(scal[1] * 8, 8)
    zero = jnp.zeros((8, 128), F32)
    z = lanes((MX, 128)) % 2 == 0

    def body(m, n):
        for t in range(n):
            v = m2[m + t]
            low, high = jnp.where(z, v, down(v, 1, 1)), jnp.where(z, up(v, 1, 1), v)
            wide[m + t, 0:8, :] = zero
            wide[m + t, 72:80, :] = zero
            for a in range(2):
                wide[m + t, pl.ds(8 + a, MX, stride=2), :] = low
                wide[m + t, pl.ds(40 + a, MX, stride=2), :] = high

    rows(lo, hi, body)

    def add(m, n):
        y = 2 * m - 32 + HALO
        new = []
        for t in range(n):
            w = wide[m + t, pl.ds(begin, FX), :]
            new += [u_ref[y + 2 * t] + w, u_ref[y + 2 * t + 1] + w]
        for t in range(2 * n):
            dst[y + t] = new[t]

    rows(lo, hi, add)


def middle_kernel(scal, src, fbx, fby, fbz, fdiag, finv, u2, here, near, swapped,
                  mbx, mby, mbz, mdiag, minv, lbx, lby, lbz, linv, u2_out, pack,
                  joined, rhs, absorb, conduct, m1, m2, lrhs, l1, l2, labsorb, lconduct, tmp, wide, fa, fb):
    fine = Level(fbx, fby, fbz, fdiag, finv, 1, False)
    mid = Level(mbx, mby, mbz, mdiag, minv, 2, True)
    low = Level(lbx, lby, lbz, None, linv, 4, True)
    gather_rows(scal, here, near, swapped, joined, 3)
    unpack_rows(joined, 0, rhs)
    unpack_rows(joined, 2, absorb)
    unpack_rows(joined, 4, conduct)
    mid.build(conduct, absorb, 2, 38, 4.0)
    restrict_low(lambda y, n: [absorb[y + t] for t in range(n)], tmp, labsorb, 1, 19)
    restrict_low(lambda y, n: [conduct[y + t] for t in range(n)], tmp, lconduct, 1, 19)
    low.build(lconduct, labsorb, 2, 18, 16.0)
    coarse(mid, low, rhs, m1, m2, lrhs, l1, l2, tmp, 0)
    prolong_add(scal, m2, wide, u2, fa, 12, 28)
    fine.sweep(fb, fa, src, 3, ROWS - 3)
    fine.sweep(fa, fb, src, 4, ROWS - 4)
    fine.sweep(fb, fa, src, 5, ROWS - 5)
    zero = jnp.zeros((FX, 128), F32)
    for y in (*range(6), *range(ROWS - 6, ROWS)):
        u2_out[y] = zero
    fine.sweep(u2_out, fb, src, 6, ROWS - 6)
    tiles = restrict_own([r[8:16] for r in fine.residual(u2_out, src, HALO, 16)])
    for i, t in enumerate(tiles):
        pack[i] = t


def last_kernel(scal, src, fbx, fby, fbz, fdiag, finv, u2, here, near, swapped,
                mbx, mby, mbz, mdiag, minv, lbx, lby, lbz, linv,
                out, out_res,
                joined, rhs, m1, m2, lrhs, l1, l2, tmp, wide, fa, fb):
    fine = Level(fbx, fby, fbz, fdiag, finv, 1, False)
    mid = Level(mbx, mby, mbz, mdiag, minv, 2, True)
    low = Level(lbx, lby, lbz, None, linv, 4, True)
    gather_rows(scal, here, near, swapped, joined, 1)
    unpack_rows(joined, 0, rhs)
    coarse(mid, low, rhs, m1, m2, lrhs, l1, l2, tmp, 1)
    prolong_add(scal, m2, wide, u2, fa, 14, 26)
    fine.sweep(fb, fa, src, 7, ROWS - 7)
    fine.sweep(fa, fb, src, 8, ROWS - 8)

    def finish(y, n):
        r = fine.residual(fa, src, HALO + y, n)
        for t in range(n):
            at = pl.ds(y + t, 8, stride=16)
            out[at, :] = fa[HALO + y + t, 8:16, :]
            out_res[at, :] = r[t][8:16]

    rows(0, 16, finish)


def call(kernel, outs, scratch, *args):
    return pl.pallas_call(
        kernel,
        out_shape=[jax.ShapeDtypeStruct(s, F32) for s in outs],
        in_specs=[pl.BlockSpec(memory_space=pltpu.SMEM)]
        + [pl.BlockSpec(memory_space=pltpu.VMEM)] * (len(args) - 1),
        out_specs=[pl.BlockSpec(memory_space=pltpu.VMEM)] * len(outs),
        scratch_shapes=[pltpu.VMEM(s, F32) for s in scratch],
        compiler_params=pltpu.CompilerParams(vmem_limit_bytes=VMEM_LIMIT),
    )(*args)


def other_core(array):
    return lax.ppermute(array, "dev", [(i, i ^ 1) for i in range(8)])


def one_away(g, core):
    return 1 if g % 2 == core else -1


def two_away(g, core):
    return 2 if g // 2 % 2 != core else -2


def spread(pack):
    peers, devs = lax.axis_size("grp"), lax.axis_size("dev")

    def from_beside(array, by):
        pairs = []
        for g in range(peers):
            for d in range(devs):
                there = g + by(g, d % 2)
                if 0 <= there < peers:
                    pairs.append((there * devs + d, g * devs + d))
        return lax.ppermute(array, ("grp", "dev"), pairs)

    here = lax.all_to_all(jnp.broadcast_to(pack, (devs,) + pack.shape), "dev", 0, 0)
    near = jnp.stack([from_beside(here, one_away), from_beside(here, two_away)])
    return here, near, other_core(near)


def local(source, absorb, conduct):
    peers = lax.axis_size("grp")
    d = lax.axis_index("dev")
    g, core = lax.axis_index("grp"), d % 2
    scal = jnp.stack([core, d, g % 2 == core, g // 2 % 2 != core]).astype(jnp.int32)

    fine = jnp.stack([source, absorb, conduct]).transpose(0, 2, 1, 3)
    even = g % 2 == 0
    first, last = fine[:, :HALO], fine[:, 16 - HALO:]

    def swap_rows(array, low):
        pairs = [(i, i + 1) for i in range(low, peers - 1, 2)]
        return lax.ppermute(array, "grp", pairs + [(j, i) for i, j in pairs])

    one = swap_rows(jnp.where(even, last, first), 0)
    two = swap_rows(jnp.where(even, first, last), 1)
    before, after = jnp.where(even, two, one), jnp.where(even, one, two)
    fine = jnp.concatenate([before, fine, after], axis=1)

    def other_chip(array):
        return lax.ppermute(array, "dev", [(1, 2), (2, 1), (3, 4), (4, 3), (5, 6), (6, 5)])

    one, two = fine[:, HALO - 3:ROWS - HALO + 3:2], fine[:, HALO - 2:ROWS - HALO + 3:2]
    near = [jnp.concatenate([one[:, :, x:x + 4], two[:, :, x:x + 4]], axis=2) for x in (0, 4)]
    near_a = other_core(jnp.where(core == 0, near[1], near[0]))
    near_b = other_chip(jnp.where(core == 0, near[0], near[1]))
    block, wide_mid, wide_low = (ROWS, FX, 128), (MROWS, MX, 128), (LROWS, LX, 128)
    pack, ends = call(first_kernel, [(6, 8, 128), (2, 16, 128)], [block] * 9, scal, fine, near_a, near_b)
    parts = spread(pack)
    whole, ends = fine.reshape(3 * ROWS, 8, 128), ends.reshape(2, 2, 8, 128)
    via_a = other_core(jnp.concatenate([whole, jnp.where(core == 0, ends[0], ends[1])]))
    via_b = other_chip(jnp.concatenate([whole, jnp.where(core == 0, ends[1], ends[0])]))
    *state, u2 = call(rim_kernel, [block] * 7, [block] * 3, scal, fine, via_a, via_b)
    *coefs, u2, pack = call(
        middle_kernel,
        [wide_mid] * 5 + [wide_low] * 4 + [block, (2, 8, 128)],
        [(5, 6, 64, 128)] + [wide_mid] * 5 + [wide_low] * 5 + [(20, MX, 128), (MROWS, 80, 128), block, block],
        scal, *state, u2, *parts,
    )
    parts = spread(pack)
    out, res = call(
        last_kernel,
        [(128, 128), (128, 128)],
        [(5, 2, 64, 128)] + [wide_mid] * 3 + [wide_low] * 3 + [(20, MX, 128), (MROWS, 80, 128), block, block],
        scal, *state, u2, *parts, *coefs,
    )
    return out.reshape(8, 16, 128), res.reshape(8, 16, 128)


def solution(mesh):
    spec = P("dev", "grp", None)
    return jax.shard_map(local, mesh=mesh, in_specs=(spec,) * 3, out_specs=(spec,) * 2, check_vma=False)
```

```python
import functools

import jax
import jax.numpy as jnp
from jax import lax
from jax.experimental import pallas as pl
from jax.experimental.pallas import tpu as pltpu
from jax.sharding import PartitionSpec as P

RELAX = 0.8
HALO = 9
ROWS = 16 + 2 * HALO
FX = 24
MROWS = 40
MX = 16
LROWS = 20
LX = 8
VMEM_LIMIT = 40 * 1024 * 1024

F32 = jnp.float32


def rows(lo, hi, body):
    body(lo, hi - lo)


def lanes(shape):
    return lax.broadcasted_iota(jnp.int32, shape, 1)


def planes(shape):
    return lax.broadcasted_iota(jnp.int32, shape, 0)


def up(value, axis, by):
    return pltpu.roll(value, value.shape[axis] - by, axis)


def down(value, axis, by):
    return pltpu.roll(value, by, axis)


def next_plane(value):
    value = up(value, 0, 1)
    last = value[-8:]
    last = jnp.where(planes((8, 128)) == 7, up(last, 1, 1), last)
    return last if value.shape[0] == 8 else jnp.concatenate([value[:-8], last])


def previous_plane(value):
    value = down(value, 0, 1)
    first = value[:8]
    first = jnp.where(planes((8, 128)) == 0, down(first, 1, 1), first)
    return first if value.shape[0] == 8 else jnp.concatenate([first, value[8:]])


class Level:
    def __init__(self, bx, by, bz, diag, inv, width, folded):
        self.bx, self.by, self.bz, self.diag, self.inv, self.width = bx, by, bz, diag, inv, width
        self.folded = folded
        self.next = next_plane if folded else lambda value: up(value, 0, 1)
        self.previous = previous_plane if folded else lambda value: down(value, 0, 1)

    def beside(self, u_ref, y, n):
        u = [u_ref[y - 1 + t] for t in range(n + 2)]
        by = [self.by[y - 1 + t] for t in range(n + 1)]
        flow = [by[t] * u[t + 1] for t in range(n + 1)]
        acc = []
        for t in range(n):
            here, bx, bz = u[t + 1], self.bx[y + t], self.bz[y + t]
            x = bx * self.next(here) + self.previous(bx * here)
            z = bz * up(here, 1, self.width) + down(bz * here, 1, self.width)
            acc.append((by[t] * u[t] + by[t + 1] * u[t + 2]) + (x + z))
        return u[1:-1], acc

    def sweep(self, dst, src, rhs, lo, hi):
        def body(y, n):
            u, acc = self.beside(src, y, n)
            new = [(1.0 - RELAX) * u[t] + self.inv[y + t] * (rhs[y + t] + acc[t]) for t in range(n)]
            for t in range(n):
                dst[y + t] = new[t]

        rows(lo, hi, body)

    def residual(self, u_ref, rhs, y, n):
        u, acc = self.beside(u_ref, y, n)
        return [rhs[y + t] - self.diag[y + t] * u[t] + acc[t] for t in range(n)]

    def build(self, conduct, absorb, lo, hi, spacing):
        shape = conduct.shape[1:]
        z, x = lanes(shape), planes(shape)
        half = 0.5 / spacing
        final = jnp.logical_and(x == shape[0] - 1, z % 2 == 1)
        initial = jnp.logical_and(x == 0, z % 2 == 0)

        def body(y, n):
            c = [conduct[y - 1 + t] for t in range(n + 2)]
            done = []
            for t in range(n):
                here = c[t + 1]
                xp, xm = self.next(here), self.previous(here)
                if self.folded:
                    xp = jnp.where(final, 0.0, xp)
                    xm = jnp.where(initial, 0.0, xm)
                zp = jnp.where(z >= shape[1] - self.width, 0.0, up(here, 1, self.width))
                zm = jnp.where(z < self.width, 0.0, down(here, 1, self.width))
                bx = (here + xp) * half
                if self.folded:
                    bx = jnp.where(final, 0.0, bx)
                by = (here + c[t + 2]) * half
                bz = jnp.where(z >= shape[1] - self.width, 0.0, (here + zp) * half)
                a = absorb[y + t]
                diag = a + (3.0 / spacing) * here + half * (((xp + xm) + (c[t] + c[t + 2])) + (zp + zm))
                done.append((bx, by, bz, diag, jnp.where(a > 0.0, RELAX / diag, 0.0)))
            for t in range(n):
                for ref, value in zip((self.bx, self.by, self.bz, self.diag, self.inv), done[t]):
                    if ref is not None:
                        ref[y + t] = value

        self.by[lo - 1] = (conduct[lo - 1] + conduct[lo]) * half
        rows(lo, hi, body)


def pair_lanes(t, width):
    first = (lanes(t.shape) // width) % 2 == 0
    return t + jnp.where(first, up(t, 1, width), down(t, 1, width))


def pair_planes(t):
    first = planes(t.shape) % 2 == 0
    return t + jnp.where(first, up(t, 0, 1), down(t, 0, 1))


def pack_rows(row_of):
    x, z = planes((8, 128)) % 2, lanes((8, 128)) % 2
    tiles = []
    for k in range(2):
        r = [row_of(4 * k + t) for t in range(4)]
        tiles.append(jnp.where(x == 0, jnp.where(z == 0, r[0], r[1]), jnp.where(z == 0, r[2], r[3])))
    return tiles


def restrict_own(r):
    def row_of(j):
        return pair_planes(pair_lanes(r[2 * j] + r[2 * j + 1], 1)) * 0.125

    return pack_rows(row_of)


def restrict_low(fine_rows, tmp, dst, lo, hi):
    def body(i, n):
        r = fine_rows(2 * i, 2 * n)
        for t in range(n):
            tmp[t] = r[2 * t] + r[2 * t + 1]
        for t in range(n):
            pair = tmp[t, pl.ds(0, LX, stride=2), :] + tmp[t, pl.ds(1, LX, stride=2), :]
            dst[i + t] = pair_lanes(pair, 2) * 0.125

    rows(lo, hi, body)


class FirstSweep:
    def __init__(self, level, rhs):
        self.level, self.rhs = level, rhs

    def __getitem__(self, y):
        return self.level.inv[y] * self.rhs[y]


def join_planes(scal, own, via_a, via_b, arr, dst, lo, hi):
    even = scal[0] == 0
    for y in range(lo, hi):
        a, b = via_a[arr * ROWS + y], via_b[arr * ROWS + y]
        dst[y, 0:8, :] = jnp.where(even, b, a)
        dst[y, 8:16, :] = own[arr, y]
        dst[y, 16:24, :] = jnp.where(even, a, b)


def first_kernel(scal, own, near_a, near_b, pack, ends,
                 src, absorb, conduct, bx, by, bz, diag, inv, u2):
    even = scal[0] == 0
    for arr, dst in ((0, src), (1, absorb), (2, conduct)):
        for i in range(22):
            y = HALO - 3 + i
            a, b = near_a[arr, i // 2], near_b[arr, i // 2]
            left, right = jnp.where(even, b, a), jnp.where(even, a, b)
            dst[y, 0:8, :] = down(left, 0, 4) if i % 2 == 0 else left
            dst[y, 8:16, :] = own[arr, y]
            dst[y, 16:24, :] = right if i % 2 == 0 else down(right, 0, 4)
    level = Level(bx, by, bz, diag, inv, 1, False)
    level.build(conduct, absorb, HALO - 2, ROWS - HALO + 2, 1.0)
    u1 = FirstSweep(level, src)
    for y in range(16):
        own_rows = inv[HALO + y, 8:16, :] * src[HALO + y, 8:16, :]
        ends[0, y:y + 1, :] = own_rows[0:1]
        ends[1, y:y + 1, :] = own_rows[7:8]
    level.sweep(u2, u1, src, HALO - 1, ROWS - HALO + 1)
    tiles = restrict_own([r[8:16] for r in level.residual(u2, src, HALO, 16)])
    tiles += restrict_own([absorb[HALO + i, 8:16, :] for i in range(16)])
    tiles += restrict_own([conduct[HALO + i, 8:16, :] for i in range(16)])
    for i, t in enumerate(tiles):
        pack[i] = t


def rim_kernel(scal, own, via_a, via_b,
               src, bx, by, bz, diag, inv, u2,
               absorb, conduct, u1):
    for arr, dst in ((0, src), (1, absorb), (2, conduct)):
        join_planes(scal, own, via_a, via_b, arr, dst, 0, ROWS)
    level = Level(bx, by, bz, diag, inv, 1, False)
    level.build(conduct, absorb, 1, ROWS - 1, 1.0)
    x = planes((FX, 128))
    even = scal[0] == 0
    for y in range(1, ROWS - 1):
        u = inv[y] * src[y]
        if 0 <= y - HALO < 16:
            i, at = divmod(y - HALO, 8)
            a, b = (via[3 * ROWS + i, at:at + 1, :] for via in (via_a, via_b))
            left, right = jnp.where(even, b, a), jnp.where(even, a, b)
            u = jnp.where(x == 0, left, jnp.where(x == FX - 1, right, u))
        u1[y] = u
    zero = jnp.zeros((FX, 128), F32)
    for y in (0, 1, ROWS - 2, ROWS - 1):
        u2[y] = zero
    level.sweep(u2, u1, src, 2, ROWS - 2)


def gather_rows(scal, here, near, swapped, joined, arrays):
    tiles = 2 * arrays
    held = near.shape[0] - 8
    zero = jnp.zeros((8, 128), F32)

    def one_away(j, source):
        for t in range(tiles):
            for dev in range(8):
                joined[j, t, 8 * dev:8 * dev + 8, :] = source[held + dev, t]

    def two_away(j, source):
        for t in range(tiles):
            for dev in range(held):
                at = pl.ds(pl.multiple_of(8 * (scal[4] + dev), 8) if held < 8 else 8 * dev, 8)
                joined[j, t, at, :] = source[dev, t]

    for t in range(tiles):
        for dev in range(8):
            joined[2, t, 8 * dev:8 * dev + 8, :] = here[dev, t]
            if held < 8:
                joined[0, t, 8 * dev:8 * dev + 8, :] = zero
                joined[4, t, 8 * dev:8 * dev + 8, :] = zero
    for flag, put, after, before in ((scal[2], one_away, 3, 1), (scal[3], two_away, 4, 0)):

        @pl.when(flag != 0)
        def _():
            put(after, near)
            put(before, swapped)

        @pl.when(flag == 0)
        def _():
            put(after, swapped)
            put(before, near)


def unpack_rows(joined, tile, dst):
    z = lanes((MX, 128)) % 2 == 0

    for j in range(5):
        for k in range(2):
            for a in range(2):
                v = joined[j, tile + k, pl.ds(a, 2 * MX, stride=2), :]
                v, w = v[:MX], v[MX:]
                y = j * 8 + 4 * k + 2 * a
                dst[y] = jnp.where(z, v, down(w, 1, 1))
                dst[y + 1] = jnp.where(z, up(v, 1, 1), w)


def coarse(mid, low, rhs, m1, m2, lrhs, l1, l2, tmp, k):
    mid.sweep(m2, FirstSweep(mid, rhs), rhs, 3 + 2 * k, 37 - 2 * k)
    restrict_low(functools.partial(mid.residual, m2, rhs), tmp, lrhs, 2 + k, 18 - k)
    low.sweep(l2, FirstSweep(low, lrhs), lrhs, 3 + k, 17 - k)
    low.sweep(l1, l2, lrhs, 4 + k, 16 - k)
    low.sweep(l2, l1, lrhs, 5 + k, 15 - k)

    for i in range(5 + k, 15 - k):
        v = l2[i]
        for y in (2 * i, 2 * i + 1):
            for a in range(2):
                at = pl.ds(a, LX, stride=2)
                m2[y, at, :] = m2[y, at, :] + v

    mid.sweep(m1, m2, rhs, 11 + 2 * k, 29 - 2 * k)
    mid.sweep(m2, m1, rhs, 12 + 2 * k, 28 - 2 * k)


def prolong_add(scal, m2, wide, u_ref, dst, lo, hi):
    begin = pl.multiple_of(scal[1] * 8, 8)
    zero = jnp.zeros((8, 128), F32)
    z = lanes((MX, 128)) % 2 == 0

    def body(m, n):
        for t in range(n):
            v = m2[m + t]
            low, high = jnp.where(z, v, down(v, 1, 1)), jnp.where(z, up(v, 1, 1), v)
            wide[m + t, 0:8, :] = zero
            wide[m + t, 72:80, :] = zero
            for a in range(2):
                wide[m + t, pl.ds(8 + a, MX, stride=2), :] = low
                wide[m + t, pl.ds(40 + a, MX, stride=2), :] = high

    rows(lo, hi, body)

    def add(m, n):
        y = 2 * m - 32 + HALO
        new = []
        for t in range(n):
            w = wide[m + t, pl.ds(begin, FX), :]
            new += [u_ref[y + 2 * t] + w, u_ref[y + 2 * t + 1] + w]
        for t in range(2 * n):
            dst[y + t] = new[t]

    rows(lo, hi, add)


def middle_kernel(scal, src, fbx, fby, fbz, fdiag, finv, u2, here, near, swapped,
                  mbx, mby, mbz, mdiag, minv, lbx, lby, lbz, linv, u2_out, pack,
                  joined, rhs, absorb, conduct, m1, m2, lrhs, l1, l2, labsorb, lconduct, tmp, wide, fa, fb):
    fine = Level(fbx, fby, fbz, fdiag, finv, 1, False)
    mid = Level(mbx, mby, mbz, mdiag, minv, 2, True)
    low = Level(lbx, lby, lbz, None, linv, 4, True)
    gather_rows(scal, here, near, swapped, joined, 3)
    unpack_rows(joined, 0, rhs)
    unpack_rows(joined, 2, absorb)
    unpack_rows(joined, 4, conduct)
    mid.build(conduct, absorb, 2, 38, 4.0)
    restrict_low(lambda y, n: [absorb[y + t] for t in range(n)], tmp, labsorb, 1, 19)
    restrict_low(lambda y, n: [conduct[y + t] for t in range(n)], tmp, lconduct, 1, 19)
    low.build(lconduct, labsorb, 2, 18, 16.0)
    coarse(mid, low, rhs, m1, m2, lrhs, l1, l2, tmp, 0)
    prolong_add(scal, m2, wide, u2, fa, 12, 28)
    fine.sweep(fb, fa, src, 3, ROWS - 3)
    fine.sweep(fa, fb, src, 4, ROWS - 4)
    fine.sweep(fb, fa, src, 5, ROWS - 5)
    zero = jnp.zeros((FX, 128), F32)
    for y in (*range(6), *range(ROWS - 6, ROWS)):
        u2_out[y] = zero
    fine.sweep(u2_out, fb, src, 6, ROWS - 6)
    tiles = restrict_own([r[8:16] for r in fine.residual(u2_out, src, HALO, 16)])
    for i, t in enumerate(tiles):
        pack[i] = t


def last_kernel(scal, src, fbx, fby, fbz, fdiag, finv, u2, here, near, swapped,
                mbx, mby, mbz, mdiag, minv, lbx, lby, lbz, linv,
                out, out_res,
                joined, rhs, m1, m2, lrhs, l1, l2, tmp, wide, fa, fb):
    fine = Level(fbx, fby, fbz, fdiag, finv, 1, False)
    mid = Level(mbx, mby, mbz, mdiag, minv, 2, True)
    low = Level(lbx, lby, lbz, None, linv, 4, True)
    gather_rows(scal, here, near, swapped, joined, 1)
    unpack_rows(joined, 0, rhs)
    coarse(mid, low, rhs, m1, m2, lrhs, l1, l2, tmp, 1)
    prolong_add(scal, m2, wide, u2, fa, 14, 26)
    fine.sweep(fb, fa, src, 7, ROWS - 7)
    fine.sweep(fa, fb, src, 8, ROWS - 8)

    def finish(y, n):
        r = fine.residual(fa, src, HALO + y, n)
        for t in range(n):
            at = pl.ds(y + t, 8, stride=16)
            out[at, :] = fa[HALO + y + t, 8:16, :]
            out_res[at, :] = r[t][8:16]

    rows(0, 16, finish)


def call(kernel, outs, scratch, *args):
    return pl.pallas_call(
        kernel,
        out_shape=[jax.ShapeDtypeStruct(s, F32) for s in outs],
        in_specs=[pl.BlockSpec(memory_space=pltpu.SMEM)]
        + [pl.BlockSpec(memory_space=pltpu.VMEM)] * (len(args) - 1),
        out_specs=[pl.BlockSpec(memory_space=pltpu.VMEM)] * len(outs),
        scratch_shapes=[pltpu.VMEM(s, F32) for s in scratch],
        compiler_params=pltpu.CompilerParams(vmem_limit_bytes=VMEM_LIMIT),
    )(*args)


def other_core(array):
    return lax.ppermute(array, "dev", [(i, i ^ 1) for i in range(8)])


def one_away(g, core):
    return 1 if g % 2 == core else -1


def two_away(g, core):
    return 2 if g // 2 % 2 != core else -2


def spread(pack, later=None):
    peers, devs = lax.axis_size("grp"), lax.axis_size("dev")

    def from_beside(array, by):
        pairs = []
        for g in range(peers):
            for d in range(devs):
                there = g + by(g, d % 2)
                if 0 <= there < peers:
                    pairs.append((there * devs + d, g * devs + d))
        return lax.ppermute(array, ("grp", "dev"), pairs)

    here = lax.all_to_all(jnp.broadcast_to(pack, (devs,) + pack.shape), "dev", 0, 0)
    some = here
    if later is not None:
        here, later = lax.optimization_barrier((here, later))
        some = jnp.where(lax.axis_index("dev") < 4, here[:6], here[2:])
    near = jnp.concatenate([from_beside(some, two_away), from_beside(here, one_away)])
    return later, here, near, other_core(near)


def local(source, absorb, conduct):
    peers = lax.axis_size("grp")
    d = lax.axis_index("dev")
    g, core = lax.axis_index("grp"), d % 2
    scal = jnp.stack([core, d, g % 2 == core, g // 2 % 2 != core, jnp.where(d < 4, 0, 2)]).astype(jnp.int32)

    fine = jnp.stack([source, absorb, conduct]).transpose(0, 2, 1, 3)
    even = g % 2 == 0
    first, last = fine[:, :HALO], fine[:, 16 - HALO:]

    def swap_rows(array, low):
        pairs = [(i, i + 1) for i in range(low, peers - 1, 2)]
        return lax.ppermute(array, "grp", pairs + [(j, i) for i, j in pairs])

    one = swap_rows(jnp.where(even, last, first), 0)
    two = swap_rows(jnp.where(even, first, last), 1)
    before, after = jnp.where(even, two, one), jnp.where(even, one, two)
    fine = jnp.concatenate([before, fine, after], axis=1)

    def other_chip(array):
        return lax.ppermute(array, "dev", [(1, 2), (2, 1), (3, 4), (4, 3), (5, 6), (6, 5)])

    one, two = fine[:, HALO - 3:ROWS - HALO + 3:2], fine[:, HALO - 2:ROWS - HALO + 3:2]
    near = [jnp.concatenate([one[:, :, x:x + 4], two[:, :, x:x + 4]], axis=2) for x in (0, 4)]
    near_a = other_core(jnp.where(core == 0, near[1], near[0]))
    near_b = other_chip(jnp.where(core == 0, near[0], near[1]))
    block, wide_mid, wide_low = (ROWS, FX, 128), (MROWS, MX, 128), (LROWS, LX, 128)
    pack, ends = call(first_kernel, [(6, 8, 128), (2, 16, 128)], [block] * 9, scal, fine, near_a, near_b)
    ends, *parts = spread(pack, ends)
    whole, ends = fine.reshape(3 * ROWS, 8, 128), ends.reshape(2, 2, 8, 128)
    via_a = other_core(jnp.concatenate([whole, jnp.where(core == 0, ends[0], ends[1])]))
    via_b = other_chip(jnp.concatenate([whole, jnp.where(core == 0, ends[1], ends[0])]))
    *state, u2 = call(rim_kernel, [block] * 7, [block] * 3, scal, fine, via_a, via_b)
    *coefs, u2, pack = call(
        middle_kernel,
        [wide_mid] * 5 + [wide_low] * 4 + [block, (2, 8, 128)],
        [(5, 6, 64, 128)] + [wide_mid] * 5 + [wide_low] * 5 + [(20, MX, 128), (MROWS, 80, 128), block, block],
        scal, *state, u2, *parts,
    )
    _, *parts = spread(pack)
    out, res = call(
        last_kernel,
        [(128, 128), (128, 128)],
        [(5, 2, 64, 128)] + [wide_mid] * 3 + [wide_low] * 3 + [(20, MX, 128), (MROWS, 80, 128), block, block],
        scal, *state, u2, *parts, *coefs,
    )
    return out.reshape(8, 16, 128), res.reshape(8, 16, 128)


def solution(mesh):
    spec = P("dev", "grp", None)
    return jax.shard_map(local, mesh=mesh, in_specs=(spec,) * 3, out_specs=(spec,) * 2, check_vma=False)
```

```python
import functools

import jax
import jax.numpy as jnp
from jax import lax
from jax.experimental import pallas as pl
from jax.experimental.pallas import tpu as pltpu
from jax.sharding import PartitionSpec as P

RELAX = 0.8
HALO = 9
ROWS = 16 + 2 * HALO
FX = 24
MROWS = 40
MX = 16
LROWS = 20
LX = 8
VMEM_LIMIT = 40 * 1024 * 1024

F32 = jnp.float32


def rows(lo, hi, body):
    body(lo, hi - lo)


def lanes(shape):
    return lax.broadcasted_iota(jnp.int32, shape, 1)


def planes(shape):
    return lax.broadcasted_iota(jnp.int32, shape, 0)


def up(value, axis, by):
    return pltpu.roll(value, value.shape[axis] - by, axis)


def down(value, axis, by):
    return pltpu.roll(value, by, axis)


def next_plane(value):
    value = up(value, 0, 1)
    last = value[-8:]
    last = jnp.where(planes((8, 128)) == 7, up(last, 1, 1), last)
    return last if value.shape[0] == 8 else jnp.concatenate([value[:-8], last])


def previous_plane(value):
    value = down(value, 0, 1)
    first = value[:8]
    first = jnp.where(planes((8, 128)) == 0, down(first, 1, 1), first)
    return first if value.shape[0] == 8 else jnp.concatenate([first, value[8:]])


class Level:
    def __init__(self, bx, by, bz, diag, inv, width, folded):
        self.bx, self.by, self.bz, self.diag, self.inv, self.width = bx, by, bz, diag, inv, width
        self.folded = folded
        self.next = next_plane if folded else lambda value: up(value, 0, 1)
        self.previous = previous_plane if folded else lambda value: down(value, 0, 1)

    def beside(self, u_ref, y, n):
        u = [u_ref[y - 1 + t] for t in range(n + 2)]
        by = [self.by[y - 1 + t] for t in range(n + 1)]
        flow = [by[t] * u[t + 1] for t in range(n + 1)]
        acc = []
        for t in range(n):
            here, bx, bz = u[t + 1], self.bx[y + t], self.bz[y + t]
            x = bx * self.next(here) + self.previous(bx * here)
            z = bz * up(here, 1, self.width) + down(bz * here, 1, self.width)
            acc.append((by[t] * u[t] + by[t + 1] * u[t + 2]) + (x + z))
        return u[1:-1], acc

    def sweep(self, dst, src, rhs, lo, hi):
        def body(y, n):
            u, acc = self.beside(src, y, n)
            new = [(1.0 - RELAX) * u[t] + self.inv[y + t] * (rhs[y + t] + acc[t]) for t in range(n)]
            for t in range(n):
                dst[y + t] = new[t]

        rows(lo, hi, body)

    def residual(self, u_ref, rhs, y, n):
        u, acc = self.beside(u_ref, y, n)
        return [rhs[y + t] - self.diag[y + t] * u[t] + acc[t] for t in range(n)]

    def build(self, conduct, absorb, lo, hi, spacing):
        shape = conduct.shape[1:]
        z, x = lanes(shape), planes(shape)
        half = 0.5 / spacing
        final = jnp.logical_and(x == shape[0] - 1, z % 2 == 1)
        initial = jnp.logical_and(x == 0, z % 2 == 0)

        def body(y, n):
            c = [conduct[y - 1 + t] for t in range(n + 2)]
            done = []
            for t in range(n):
                here = c[t + 1]
                xp, xm = self.next(here), self.previous(here)
                if self.folded:
                    xp = jnp.where(final, 0.0, xp)
                    xm = jnp.where(initial, 0.0, xm)
                zp = jnp.where(z >= shape[1] - self.width, 0.0, up(here, 1, self.width))
                zm = jnp.where(z < self.width, 0.0, down(here, 1, self.width))
                bx = (here + xp) * half
                if self.folded:
                    bx = jnp.where(final, 0.0, bx)
                by = (here + c[t + 2]) * half
                bz = jnp.where(z >= shape[1] - self.width, 0.0, (here + zp) * half)
                a = absorb[y + t]
                diag = a + (3.0 / spacing) * here + half * (((xp + xm) + (c[t] + c[t + 2])) + (zp + zm))
                done.append((bx, by, bz, diag, jnp.where(a > 0.0, RELAX / diag, 0.0)))
            for t in range(n):
                for ref, value in zip((self.bx, self.by, self.bz, self.diag, self.inv), done[t]):
                    if ref is not None:
                        ref[y + t] = value

        self.by[lo - 1] = (conduct[lo - 1] + conduct[lo]) * half
        rows(lo, hi, body)


def pair_lanes(t, width):
    first = (lanes(t.shape) // width) % 2 == 0
    return t + jnp.where(first, up(t, 1, width), down(t, 1, width))


def pair_planes(t):
    first = planes(t.shape) % 2 == 0
    return t + jnp.where(first, up(t, 0, 1), down(t, 0, 1))


def pack_rows(row_of):
    x, z = planes((8, 128)) % 2, lanes((8, 128)) % 2
    tiles = []
    for k in range(2):
        r = [row_of(4 * k + t) for t in range(4)]
        tiles.append(jnp.where(x == 0, jnp.where(z == 0, r[0], r[1]), jnp.where(z == 0, r[2], r[3])))
    return tiles


def restrict_own(r):
    def row_of(j):
        return pair_planes(pair_lanes(r[2 * j] + r[2 * j + 1], 1)) * 0.125

    return pack_rows(row_of)


def restrict_low(fine_rows, tmp, dst, lo, hi):
    def body(i, n):
        r = fine_rows(2 * i, 2 * n)
        for t in range(n):
            tmp[t] = r[2 * t] + r[2 * t + 1]
        for t in range(n):
            pair = tmp[t, pl.ds(0, LX, stride=2), :] + tmp[t, pl.ds(1, LX, stride=2), :]
            dst[i + t] = pair_lanes(pair, 2) * 0.125

    rows(lo, hi, body)


class FirstSweep:
    def __init__(self, level, rhs):
        self.level, self.rhs = level, rhs

    def __getitem__(self, y):
        return self.level.inv[y] * self.rhs[y]


def join_planes(scal, own, via_a, via_b, arr, dst, lo, hi):
    even = scal[0] == 0
    for y in range(lo, hi):
        a, b = via_a[arr * ROWS + y], via_b[arr * ROWS + y]
        dst[y, 0:8, :] = jnp.where(even, b, a)
        dst[y, 8:16, :] = own[arr, y]
        dst[y, 16:24, :] = jnp.where(even, a, b)


def first_kernel(scal, own, near_a, near_b, pack, ends,
                 src, absorb, conduct, bx, by, bz, diag, inv, u2):
    even = scal[0] == 0
    for arr, dst in ((0, src), (1, absorb), (2, conduct)):
        for i in range(22):
            y, half = HALO - 3 + i, 4 * (i % 2)
            a, b = near_a[arr, i // 2], near_b[arr, i // 2]
            dst[y, 0:4, :] = jnp.where(even, b, a)[half:half + 4]
            dst[y, 4:12, :] = own[arr, y]
            dst[y, 12:16, :] = jnp.where(even, a, b)[half:half + 4]
    level = Level(bx, by, bz, diag, inv, 1, False)
    level.build(conduct, absorb, HALO - 2, ROWS - HALO + 2, 1.0)
    u1 = FirstSweep(level, src)
    for y in range(16):
        own_rows = inv[HALO + y, 4:12, :] * src[HALO + y, 4:12, :]
        ends[0, y:y + 1, :] = own_rows[0:1]
        ends[1, y:y + 1, :] = own_rows[7:8]
    level.sweep(u2, u1, src, HALO - 1, ROWS - HALO + 1)
    tiles = restrict_own([r[4:12] for r in level.residual(u2, src, HALO, 16)])
    tiles += restrict_own([own[1, HALO + i] for i in range(16)])
    tiles += restrict_own([own[2, HALO + i] for i in range(16)])
    for i, t in enumerate(tiles):
        pack[i] = t


def rim_kernel(scal, own, via_a, via_b,
               src, bx, by, bz, diag, inv, u2,
               absorb, conduct, u1):
    for arr, dst in ((0, src), (1, absorb), (2, conduct)):
        join_planes(scal, own, via_a, via_b, arr, dst, 0, ROWS)
    level = Level(bx, by, bz, diag, inv, 1, False)
    level.build(conduct, absorb, 1, ROWS - 1, 1.0)
    x = planes((FX, 128))
    even = scal[0] == 0
    for y in range(1, ROWS - 1):
        u = inv[y] * src[y]
        if 0 <= y - HALO < 16:
            i, at = divmod(y - HALO, 8)
            a, b = (via[3 * ROWS + i, at:at + 1, :] for via in (via_a, via_b))
            left, right = jnp.where(even, b, a), jnp.where(even, a, b)
            u = jnp.where(x == 0, left, jnp.where(x == FX - 1, right, u))
        u1[y] = u
    zero = jnp.zeros((FX, 128), F32)
    for y in (0, 1, ROWS - 2, ROWS - 1):
        u2[y] = zero
    level.sweep(u2, u1, src, 2, ROWS - 2)


def gather_rows(scal, here, near, swapped, joined, arrays):
    def copy(j, source):
        for t in range(2 * arrays):
            for dev in range(8):
                joined[j, t, 8 * dev:8 * dev + 8, :] = source[dev, t]

    copy(2, here)
    for i in range(2):
        after, before = 3 + i, 1 - i
        near_after = scal[2 + i] != 0

        @pl.when(near_after)
        def _():
            copy(after, near.at[i])
            copy(before, swapped.at[i])

        @pl.when(jnp.logical_not(near_after))
        def _():
            copy(after, swapped.at[i])
            copy(before, near.at[i])


def unpack_rows(joined, tile, dst):
    z = lanes((MX, 128)) % 2 == 0

    for j in range(5):
        for k in range(2):
            for a in range(2):
                v = joined[j, tile + k, pl.ds(a, 2 * MX, stride=2), :]
                v, w = v[:MX], v[MX:]
                y = j * 8 + 4 * k + 2 * a
                dst[y] = jnp.where(z, v, down(w, 1, 1))
                dst[y + 1] = jnp.where(z, up(v, 1, 1), w)


def coarse(mid, low, rhs, m1, m2, lrhs, l1, l2, tmp, k):
    mid.sweep(m2, FirstSweep(mid, rhs), rhs, 3 + 2 * k, 37 - 2 * k)
    restrict_low(functools.partial(mid.residual, m2, rhs), tmp, lrhs, 2 + k, 18 - k)
    low.sweep(l2, FirstSweep(low, lrhs), lrhs, 3 + k, 17 - k)
    low.sweep(l1, l2, lrhs, 4 + k, 16 - k)
    low.sweep(l2, l1, lrhs, 5 + k, 15 - k)

    for i in range(5 + k, 15 - k):
        v = l2[i]
        for y in (2 * i, 2 * i + 1):
            for a in range(2):
                at = pl.ds(a, LX, stride=2)
                m2[y, at, :] = m2[y, at, :] + v

    mid.sweep(m1, m2, rhs, 11 + 2 * k, 29 - 2 * k)
    mid.sweep(m2, m1, rhs, 12 + 2 * k, 28 - 2 * k)


def prolong_add(scal, m2, wide, u_ref, dst, lo, hi):
    begin = pl.multiple_of(scal[1] * 8, 8)
    zero = jnp.zeros((8, 128), F32)
    z = lanes((MX, 128)) % 2 == 0

    def body(m, n):
        for t in range(n):
            v = m2[m + t]
            low, high = jnp.where(z, v, down(v, 1, 1)), jnp.where(z, up(v, 1, 1), v)
            wide[m + t, 0:8, :] = zero
            wide[m + t, 72:80, :] = zero
            for a in range(2):
                wide[m + t, pl.ds(8 + a, MX, stride=2), :] = low
                wide[m + t, pl.ds(40 + a, MX, stride=2), :] = high

    rows(lo, hi, body)

    def add(m, n):
        y = 2 * m - 32 + HALO
        new = []
        for t in range(n):
            w = wide[m + t, pl.ds(begin, FX), :]
            new += [u_ref[y + 2 * t] + w, u_ref[y + 2 * t + 1] + w]
        for t in range(2 * n):
            dst[y + t] = new[t]

    rows(lo, hi, add)


def middle_kernel(scal, src, fbx, fby, fbz, fdiag, finv, u2, here, near, swapped,
                  mbx, mby, mbz, mdiag, minv, lbx, lby, lbz, linv, u2_out, pack,
                  joined, rhs, absorb, conduct, m1, m2, lrhs, l1, l2, labsorb, lconduct, tmp, wide, fa, fb):
    fine = Level(fbx, fby, fbz, fdiag, finv, 1, False)
    mid = Level(mbx, mby, mbz, mdiag, minv, 2, True)
    low = Level(lbx, lby, lbz, None, linv, 4, True)
    gather_rows(scal, here, near, swapped, joined, 3)
    unpack_rows(joined, 0, rhs)
    unpack_rows(joined, 2, absorb)
    unpack_rows(joined, 4, conduct)
    mid.build(conduct, absorb, 2, 38, 4.0)
    restrict_low(lambda y, n: [absorb[y + t] for t in range(n)], tmp, labsorb, 1, 19)
    restrict_low(lambda y, n: [conduct[y + t] for t in range(n)], tmp, lconduct, 1, 19)
    low.build(lconduct, labsorb, 2, 18, 16.0)
    coarse(mid, low, rhs, m1, m2, lrhs, l1, l2, tmp, 0)
    prolong_add(scal, m2, wide, u2, fa, 12, 28)
    fine.sweep(fb, fa, src, 3, ROWS - 3)
    fine.sweep(fa, fb, src, 4, ROWS - 4)
    fine.sweep(fb, fa, src, 5, ROWS - 5)
    zero = jnp.zeros((FX, 128), F32)
    for y in (*range(6), *range(ROWS - 6, ROWS)):
        u2_out[y] = zero
    fine.sweep(u2_out, fb, src, 6, ROWS - 6)
    tiles = restrict_own([r[8:16] for r in fine.residual(u2_out, src, HALO, 16)])
    for i, t in enumerate(tiles):
        pack[i] = t


def last_kernel(scal, src, fbx, fby, fbz, fdiag, finv, u2, here, near, swapped,
                mbx, mby, mbz, mdiag, minv, lbx, lby, lbz, linv,
                out, out_res,
                joined, rhs, m1, m2, lrhs, l1, l2, tmp, wide, fa, fb):
    fine = Level(fbx, fby, fbz, fdiag, finv, 1, False)
    mid = Level(mbx, mby, mbz, mdiag, minv, 2, True)
    low = Level(lbx, lby, lbz, None, linv, 4, True)
    gather_rows(scal, here, near, swapped, joined, 1)
    unpack_rows(joined, 0, rhs)
    coarse(mid, low, rhs, m1, m2, lrhs, l1, l2, tmp, 1)
    prolong_add(scal, m2, wide, u2, fa, 14, 26)
    fine.sweep(fb, fa, src, 7, ROWS - 7)
    fine.sweep(fa, fb, src, 8, ROWS - 8)

    def finish(y, n):
        r = fine.residual(fa, src, HALO + y, n)
        for t in range(n):
            at = pl.ds(y + t, 8, stride=16)
            out[at, :] = fa[HALO + y + t, 8:16, :]
            out_res[at, :] = r[t][8:16]

    rows(0, 16, finish)


def call(kernel, outs, scratch, *args):
    return pl.pallas_call(
        kernel,
        out_shape=[jax.ShapeDtypeStruct(s, F32) for s in outs],
        in_specs=[pl.BlockSpec(memory_space=pltpu.SMEM)]
        + [pl.BlockSpec(memory_space=pltpu.VMEM)] * (len(args) - 1),
        out_specs=[pl.BlockSpec(memory_space=pltpu.VMEM)] * len(outs),
        scratch_shapes=[pltpu.VMEM(s, F32) for s in scratch],
        compiler_params=pltpu.CompilerParams(vmem_limit_bytes=VMEM_LIMIT),
    )(*args)


def other_core(array):
    return lax.ppermute(array, "dev", [(i, i ^ 1) for i in range(8)])


def one_away(g, core):
    return 1 if g % 2 == core else -1


def two_away(g, core):
    return 2 if g // 2 % 2 != core else -2


def spread(pack):
    peers, devs = lax.axis_size("grp"), lax.axis_size("dev")

    def from_beside(array, by):
        pairs = []
        for g in range(peers):
            for d in range(devs):
                there = g + by(g, d % 2)
                if 0 <= there < peers:
                    pairs.append((there * devs + d, g * devs + d))
        return lax.ppermute(array, ("grp", "dev"), pairs)

    here = lax.all_to_all(jnp.broadcast_to(pack, (devs,) + pack.shape), "dev", 0, 0)
    near = jnp.stack([from_beside(here, one_away), from_beside(here, two_away)])
    return here, near, other_core(near)


def local(source, absorb, conduct):
    peers = lax.axis_size("grp")
    d = lax.axis_index("dev")
    g, core = lax.axis_index("grp"), d % 2
    scal = jnp.stack([core, d, g % 2 == core, g // 2 % 2 != core]).astype(jnp.int32)

    fine = jnp.stack([source, absorb, conduct]).transpose(0, 2, 1, 3)
    even = g % 2 == 0
    first, last = fine[:, :HALO], fine[:, 16 - HALO:]

    def swap_rows(array, low):
        pairs = [(i, i + 1) for i in range(low, peers - 1, 2)]
        return lax.ppermute(array, "grp", pairs + [(j, i) for i, j in pairs])

    one = swap_rows(jnp.where(even, last, first), 0)
    two = swap_rows(jnp.where(even, first, last), 1)
    before, after = jnp.where(even, two, one), jnp.where(even, one, two)
    fine = jnp.concatenate([before, fine, after], axis=1)

    def other_chip(array):
        return lax.ppermute(array, "dev", [(1, 2), (2, 1), (3, 4), (4, 3), (5, 6), (6, 5)])

    one, two = fine[:, HALO - 3:ROWS - HALO + 3:2], fine[:, HALO - 2:ROWS - HALO + 3:2]
    near = [jnp.concatenate([one[:, :, x:x + 4], two[:, :, x:x + 4]], axis=2) for x in (0, 4)]
    near_a = other_core(jnp.where(core == 0, near[1], near[0]))
    near_b = other_chip(jnp.where(core == 0, near[0], near[1]))
    block, wide_mid, wide_low = (ROWS, FX, 128), (MROWS, MX, 128), (LROWS, LX, 128)
    pack, ends = call(first_kernel, [(6, 8, 128), (2, 16, 128)], [(ROWS, 16, 128)] * 9, scal, fine, near_a, near_b)
    parts = spread(pack)
    whole, ends = fine.reshape(3 * ROWS, 8, 128), ends.reshape(2, 2, 8, 128)
    via_a = other_core(jnp.concatenate([whole, jnp.where(core == 0, ends[0], ends[1])]))
    via_b = other_chip(jnp.concatenate([whole, jnp.where(core == 0, ends[1], ends[0])]))
    *state, u2 = call(rim_kernel, [block] * 7, [block] * 3, scal, fine, via_a, via_b)
    *coefs, u2, pack = call(
        middle_kernel,
        [wide_mid] * 5 + [wide_low] * 4 + [block, (2, 8, 128)],
        [(5, 6, 64, 128)] + [wide_mid] * 5 + [wide_low] * 5 + [(20, MX, 128), (MROWS, 80, 128), block, block],
        scal, *state, u2, *parts,
    )
    parts = spread(pack)
    out, res = call(
        last_kernel,
        [(128, 128), (128, 128)],
        [(5, 2, 64, 128)] + [wide_mid] * 3 + [wide_low] * 3 + [(20, MX, 128), (MROWS, 80, 128), block, block],
        scal, *state, u2, *parts, *coefs,
    )
    return out.reshape(8, 16, 128), res.reshape(8, 16, 128)


def solution(mesh):
    spec = P("dev", "grp", None)
    return jax.shard_map(local, mesh=mesh, in_specs=(spec,) * 3, out_specs=(spec,) * 2, check_vma=False)
```

```python
import functools

import jax
import jax.numpy as jnp
from jax import lax
from jax.experimental import pallas as pl
from jax.experimental.pallas import tpu as pltpu
from jax.sharding import PartitionSpec as P

RELAX = 0.8
HALO = 9
ROWS = 16 + 2 * HALO
FX = 24
MROWS = 40
MX = 16
LROWS = 20
LX = 8
VMEM_LIMIT = 40 * 1024 * 1024

F32 = jnp.float32


def rows(lo, hi, body):
    body(lo, hi - lo)


def lanes(shape):
    return lax.broadcasted_iota(jnp.int32, shape, 1)


def planes(shape):
    return lax.broadcasted_iota(jnp.int32, shape, 0)


def up(value, axis, by):
    return pltpu.roll(value, value.shape[axis] - by, axis)


def down(value, axis, by):
    return pltpu.roll(value, by, axis)


def next_plane(value):
    value = up(value, 0, 1)
    last = value[-8:]
    last = jnp.where(planes((8, 128)) == 7, up(last, 1, 1), last)
    return last if value.shape[0] == 8 else jnp.concatenate([value[:-8], last])


def previous_plane(value):
    value = down(value, 0, 1)
    first = value[:8]
    first = jnp.where(planes((8, 128)) == 0, down(first, 1, 1), first)
    return first if value.shape[0] == 8 else jnp.concatenate([first, value[8:]])


class Level:
    def __init__(self, bx, by, bz, diag, inv, width, folded):
        self.bx, self.by, self.bz, self.diag, self.inv, self.width = bx, by, bz, diag, inv, width
        self.folded = folded
        self.next = next_plane if folded else lambda value: up(value, 0, 1)
        self.previous = previous_plane if folded else lambda value: down(value, 0, 1)

    def beside(self, u_ref, y, n):
        u = [u_ref[y - 1 + t] for t in range(n + 2)]
        by = [self.by[y - 1 + t] for t in range(n + 1)]
        flow = [by[t] * u[t + 1] for t in range(n + 1)]
        acc = []
        for t in range(n):
            here, bx, bz = u[t + 1], self.bx[y + t], self.bz[y + t]
            x = bx * self.next(here) + self.previous(bx * here)
            z = bz * up(here, 1, self.width) + down(bz * here, 1, self.width)
            acc.append((by[t] * u[t] + by[t + 1] * u[t + 2]) + (x + z))
        return u[1:-1], acc

    def sweep(self, dst, src, rhs, lo, hi):
        def body(y, n):
            u, acc = self.beside(src, y, n)
            new = [(1.0 - RELAX) * u[t] + self.inv[y + t] * (rhs[y + t] + acc[t]) for t in range(n)]
            for t in range(n):
                dst[y + t] = new[t]

        rows(lo, hi, body)

    def residual(self, u_ref, rhs, y, n):
        u, acc = self.beside(u_ref, y, n)
        return [rhs[y + t] - self.diag[y + t] * u[t] + acc[t] for t in range(n)]

    def build(self, conduct, absorb, lo, hi, spacing):
        shape = conduct.shape[1:]
        z, x = lanes(shape), planes(shape)
        half = 0.5 / spacing
        final = jnp.logical_and(x == shape[0] - 1, z % 2 == 1)
        initial = jnp.logical_and(x == 0, z % 2 == 0)

        def body(y, n):
            c = [conduct[y - 1 + t] for t in range(n + 2)]
            done = []
            for t in range(n):
                here = c[t + 1]
                xp, xm = self.next(here), self.previous(here)
                if self.folded:
                    xp = jnp.where(final, 0.0, xp)
                    xm = jnp.where(initial, 0.0, xm)
                zp = jnp.where(z >= shape[1] - self.width, 0.0, up(here, 1, self.width))
                zm = jnp.where(z < self.width, 0.0, down(here, 1, self.width))
                bx = (here + xp) * half
                if self.folded:
                    bx = jnp.where(final, 0.0, bx)
                by = (here + c[t + 2]) * half
                bz = jnp.where(z >= shape[1] - self.width, 0.0, (here + zp) * half)
                a = absorb[y + t]
                diag = a + (3.0 / spacing) * here + half * (((xp + xm) + (c[t] + c[t + 2])) + (zp + zm))
                done.append((bx, by, bz, diag, jnp.where(a > 0.0, RELAX / diag, 0.0)))
            for t in range(n):
                for ref, value in zip((self.bx, self.by, self.bz, self.diag, self.inv), done[t]):
                    if ref is not None:
                        ref[y + t] = value

        self.by[lo - 1] = (conduct[lo - 1] + conduct[lo]) * half
        rows(lo, hi, body)


def pair_lanes(t, width):
    first = (lanes(t.shape) // width) % 2 == 0
    return t + jnp.where(first, up(t, 1, width), down(t, 1, width))


def pair_planes(t):
    first = planes(t.shape) % 2 == 0
    return t + jnp.where(first, up(t, 0, 1), down(t, 0, 1))


def pack_rows(row_of):
    x, z = planes((8, 128)) % 2, lanes((8, 128)) % 2
    tiles = []
    for k in range(2):
        r = [row_of(4 * k + t) for t in range(4)]
        tiles.append(jnp.where(x == 0, jnp.where(z == 0, r[0], r[1]), jnp.where(z == 0, r[2], r[3])))
    return tiles


def restrict_own(r):
    def row_of(j):
        return pair_planes(pair_lanes(r[2 * j] + r[2 * j + 1], 1)) * 0.125

    return pack_rows(row_of)


def restrict_low(fine_rows, tmp, dst, lo, hi):
    def body(i, n):
        r = fine_rows(2 * i, 2 * n)
        for t in range(n):
            tmp[t] = r[2 * t] + r[2 * t + 1]
        for t in range(n):
            pair = tmp[t, pl.ds(0, LX, stride=2), :] + tmp[t, pl.ds(1, LX, stride=2), :]
            dst[i + t] = pair_lanes(pair, 2) * 0.125

    rows(lo, hi, body)


class FirstSweep:
    def __init__(self, level, rhs):
        self.level, self.rhs = level, rhs

    def __getitem__(self, y):
        return self.level.inv[y] * self.rhs[y]


def join_planes(scal, own, via_a, via_b, arr, dst, lo, hi):
    even = scal[0] == 0
    for y in range(lo, hi):
        a, b = via_a[arr * ROWS + y], via_b[arr * ROWS + y]
        dst[y, 0:8, :] = jnp.where(even, b, a)
        dst[y, 8:16, :] = own[arr, y]
        dst[y, 16:24, :] = jnp.where(even, a, b)


def first_kernel(scal, own, near_a, near_b, pack, ends,
                 src, absorb, conduct, bx, by, bz, diag, inv, u2):
    even = scal[0] == 0
    for arr, dst in ((0, src), (1, absorb), (2, conduct)):
        for i in range(22):
            y, half = HALO - 3 + i, 4 * (i % 2)
            a, b = near_a[arr, i // 2], near_b[arr, i // 2]
            dst[y, 0:4, :] = jnp.where(even, b, a)[half:half + 4]
            dst[y, 4:12, :] = own[arr, y]
            dst[y, 12:16, :] = jnp.where(even, a, b)[half:half + 4]
    level = Level(bx, by, bz, diag, inv, 1, False)
    level.build(conduct, absorb, HALO - 2, ROWS - HALO + 2, 1.0)
    u1 = FirstSweep(level, src)
    for y in range(16):
        own_rows = inv[HALO + y, 4:12, :] * src[HALO + y, 4:12, :]
        ends[0, y:y + 1, :] = own_rows[0:1]
        ends[1, y:y + 1, :] = own_rows[7:8]
    level.sweep(u2, u1, src, HALO - 1, ROWS - HALO + 1)
    tiles = restrict_own([r[4:12] for r in level.residual(u2, src, HALO, 16)])
    tiles += restrict_own([own[1, HALO + i] for i in range(16)])
    tiles += restrict_own([own[2, HALO + i] for i in range(16)])
    for i, t in enumerate(tiles):
        pack[i] = t


def rim_kernel(scal, own, via_a, via_b,
               src, bx, by, bz, diag, inv, u2,
               absorb, conduct, u1):
    for arr, dst in ((0, src), (1, absorb), (2, conduct)):
        join_planes(scal, own, via_a, via_b, arr, dst, 0, ROWS)
    level = Level(bx, by, bz, diag, inv, 1, False)
    level.build(conduct, absorb, 1, ROWS - 1, 1.0)
    x = planes((FX, 128))
    even = scal[0] == 0
    for y in range(1, ROWS - 1):
        u = inv[y] * src[y]
        if 0 <= y - HALO < 16:
            i, at = divmod(y - HALO, 8)
            a, b = (via[3 * ROWS + i, at:at + 1, :] for via in (via_a, via_b))
            left, right = jnp.where(even, b, a), jnp.where(even, a, b)
            u = jnp.where(x == 0, left, jnp.where(x == FX - 1, right, u))
        u1[y] = u
    zero = jnp.zeros((FX, 128), F32)
    for y in (0, 1, ROWS - 2, ROWS - 1):
        u2[y] = zero
    level.sweep(u2, u1, src, 2, ROWS - 2)


def gather_rows(scal, here, near, swapped, joined, arrays):
    def copy(j, source):
        for t in range(2 * arrays):
            for dev in range(8):
                joined[j, t, 8 * dev:8 * dev + 8, :] = source[dev, t]

    copy(2, here)
    for i in range(2):
        after, before = 3 + i, 1 - i
        near_after = scal[2 + i] != 0

        @pl.when(near_after)
        def _():
            copy(after, near.at[i])
            copy(before, swapped.at[i])

        @pl.when(jnp.logical_not(near_after))
        def _():
            copy(after, swapped.at[i])
            copy(before, near.at[i])


def unpack_rows(joined, tile, dst):
    z = lanes((MX, 128)) % 2 == 0

    for j in range(5):
        for k in range(2):
            for a in range(2):
                v = joined[j, tile + k, pl.ds(a, 2 * MX, stride=2), :]
                v, w = v[:MX], v[MX:]
                y = j * 8 + 4 * k + 2 * a
                dst[y] = jnp.where(z, v, down(w, 1, 1))
                dst[y + 1] = jnp.where(z, up(v, 1, 1), w)


def coarse(mid, low, rhs, m1, m2, lrhs, l1, l2, tmp, k):
    mid.sweep(m2, FirstSweep(mid, rhs), rhs, 3 + 2 * k, 37 - 2 * k)
    restrict_low(functools.partial(mid.residual, m2, rhs), tmp, lrhs, 2 + k, 18 - k)
    low.sweep(l2, FirstSweep(low, lrhs), lrhs, 3 + k, 17 - k)
    low.sweep(l1, l2, lrhs, 4 + k, 16 - k)
    low.sweep(l2, l1, lrhs, 5 + k, 15 - k)

    for i in range(5 + k, 15 - k):
        v = l2[i]
        for y in (2 * i, 2 * i + 1):
            for a in range(2):
                at = pl.ds(a, LX, stride=2)
                m2[y, at, :] = m2[y, at, :] + v

    mid.sweep(m1, m2, rhs, 11 + 2 * k, 29 - 2 * k)
    mid.sweep(m2, m1, rhs, 12 + 2 * k, 28 - 2 * k)


def prolong_add(scal, m2, wide, u_ref, dst, lo, hi):
    begin = pl.multiple_of(scal[1] * 8, 8)
    zero = jnp.zeros((8, 128), F32)
    z = lanes((MX, 128)) % 2 == 0

    def body(m, n):
        for t in range(n):
            v = m2[m + t]
            low, high = jnp.where(z, v, down(v, 1, 1)), jnp.where(z, up(v, 1, 1), v)
            wide[m + t, 0:8, :] = zero
            wide[m + t, 72:80, :] = zero
            for a in range(2):
                wide[m + t, pl.ds(8 + a, MX, stride=2), :] = low
                wide[m + t, pl.ds(40 + a, MX, stride=2), :] = high

    rows(lo, hi, body)

    def add(m, n):
        y = 2 * m - 32 + HALO
        new = []
        for t in range(n):
            w = wide[m + t, pl.ds(begin, FX), :]
            new += [u_ref[y + 2 * t] + w, u_ref[y + 2 * t + 1] + w]
        for t in range(2 * n):
            dst[y + t] = new[t]

    rows(lo, hi, add)


def middle_kernel(scal, src, fbx, fby, fbz, fdiag, finv, u2, here, near, swapped,
                  mbx, mby, mbz, mdiag, minv, lbx, lby, lbz, linv, u2_out, pack,
                  joined, rhs, absorb, conduct, m1, m2, lrhs, l1, l2, labsorb, lconduct, tmp, wide, fa, fb):
    fine = Level(fbx, fby, fbz, fdiag, finv, 1, False)
    mid = Level(mbx, mby, mbz, mdiag, minv, 2, True)
    low = Level(lbx, lby, lbz, None, linv, 4, True)
    gather_rows(scal, here, near, swapped, joined, 3)
    unpack_rows(joined, 0, rhs)
    unpack_rows(joined, 2, absorb)
    unpack_rows(joined, 4, conduct)
    mid.build(conduct, absorb, 2, 38, 4.0)
    restrict_low(lambda y, n: [absorb[y + t] for t in range(n)], tmp, labsorb, 1, 19)
    restrict_low(lambda y, n: [conduct[y + t] for t in range(n)], tmp, lconduct, 1, 19)
    low.build(lconduct, labsorb, 2, 18, 16.0)
    coarse(mid, low, rhs, m1, m2, lrhs, l1, l2, tmp, 0)
    prolong_add(scal, m2, wide, u2, fa, 12, 28)
    fine.sweep(fb, fa, src, 3, ROWS - 3)
    fine.sweep(fa, fb, src, 4, ROWS - 4)
    fine.sweep(fb, fa, src, 5, ROWS - 5)
    zero = jnp.zeros((FX, 128), F32)
    for y in (*range(6), *range(ROWS - 6, ROWS)):
        u2_out[y] = zero
    fine.sweep(u2_out, fb, src, 6, ROWS - 6)
    tiles = restrict_own([r[8:16] for r in fine.residual(u2_out, src, HALO, 16)])
    for i, t in enumerate(tiles):
        pack[i] = t


def last_kernel(scal, src, fbx, fby, fbz, fdiag, finv, u2, here, near, swapped,
                mbx, mby, mbz, mdiag, minv, lbx, lby, lbz, linv,
                out, out_res,
                joined, rhs, m1, m2, lrhs, l1, l2, tmp, wide, fa, fb):
    fine = Level(fbx, fby, fbz, fdiag, finv, 1, False)
    mid = Level(mbx, mby, mbz, mdiag, minv, 2, True)
    low = Level(lbx, lby, lbz, None, linv, 4, True)
    gather_rows(scal, here, near, swapped, joined, 1)
    unpack_rows(joined, 0, rhs)
    coarse(mid, low, rhs, m1, m2, lrhs, l1, l2, tmp, 1)
    prolong_add(scal, m2, wide, u2, fa, 14, 26)
    fine.sweep(fb, fa, src, 7, ROWS - 7)
    fine.sweep(fa, fb, src, 8, ROWS - 8)

    def finish(y, n):
        r = fine.residual(fa, src, HALO + y, n)
        for t in range(n):
            at = pl.ds(y + t, 8, stride=16)
            out[at, :] = fa[HALO + y + t, 8:16, :]
            out_res[at, :] = r[t][8:16]

    rows(0, 16, finish)


def call(kernel, outs, scratch, *args):
    return pl.pallas_call(
        kernel,
        out_shape=[jax.ShapeDtypeStruct(s, F32) for s in outs],
        in_specs=[pl.BlockSpec(memory_space=pltpu.SMEM)]
        + [pl.BlockSpec(memory_space=pltpu.VMEM)] * (len(args) - 1),
        out_specs=[pl.BlockSpec(memory_space=pltpu.VMEM)] * len(outs),
        scratch_shapes=[pltpu.VMEM(s, F32) for s in scratch],
        compiler_params=pltpu.CompilerParams(vmem_limit_bytes=VMEM_LIMIT),
    )(*args)


def other_core(array):
    return lax.ppermute(array, "dev", [(i, i ^ 1) for i in range(8)])


def one_away(g, core):
    return 1 if g % 2 == core else -1


def two_away(g, core):
    return 2 if g // 2 % 2 == core else -2


def spread(pack):
    peers, devs = lax.axis_size("grp"), lax.axis_size("dev")

    def from_beside(array, by):
        pairs = []
        for g in range(peers):
            for d in range(devs):
                there = g + by(g, d % 2)
                if 0 <= there < peers:
                    pairs.append((there * devs + d, g * devs + d))
        return lax.ppermute(array, ("grp", "dev"), pairs)

    here = lax.all_to_all(jnp.broadcast_to(pack, (devs,) + pack.shape), "dev", 0, 0)
    near = jnp.stack([from_beside(here, one_away), from_beside(here, two_away)])
    return here, near, other_core(near)


def local(source, absorb, conduct):
    peers = lax.axis_size("grp")
    d = lax.axis_index("dev")
    g, core = lax.axis_index("grp"), d % 2
    scal = jnp.stack([core, d, g % 2 == core, g // 2 % 2 == core]).astype(jnp.int32)

    fine = jnp.stack([source, absorb, conduct]).transpose(0, 2, 1, 3)
    even = g % 2 == 0
    first, last = fine[:, :HALO], fine[:, 16 - HALO:]

    def swap_rows(array, low):
        pairs = [(i, i + 1) for i in range(low, peers - 1, 2)]
        return lax.ppermute(array, "grp", pairs + [(j, i) for i, j in pairs])

    one = swap_rows(jnp.where(even, last, first), 0)
    two = swap_rows(jnp.where(even, first, last), 1)
    before, after = jnp.where(even, two, one), jnp.where(even, one, two)
    fine = jnp.concatenate([before, fine, after], axis=1)

    def other_chip(array):
        return lax.ppermute(array, "dev", [(1, 2), (2, 1), (3, 4), (4, 3), (5, 6), (6, 5)])

    one, two = fine[:, HALO - 3:ROWS - HALO + 3:2], fine[:, HALO - 2:ROWS - HALO + 3:2]
    near = [jnp.concatenate([one[:, :, x:x + 4], two[:, :, x:x + 4]], axis=2) for x in (0, 4)]
    near_a = other_core(jnp.where(core == 0, near[1], near[0]))
    near_b = other_chip(jnp.where(core == 0, near[0], near[1]))
    block, wide_mid, wide_low = (ROWS, FX, 128), (MROWS, MX, 128), (LROWS, LX, 128)
    pack, ends = call(first_kernel, [(6, 8, 128), (2, 16, 128)], [(ROWS, 16, 128)] * 9, scal, fine, near_a, near_b)
    parts = spread(pack)
    whole, ends = fine.reshape(3 * ROWS, 8, 128), ends.reshape(2, 2, 8, 128)
    via_a = other_core(jnp.concatenate([whole, jnp.where(core == 0, ends[0], ends[1])]))
    via_b = other_chip(jnp.concatenate([whole, jnp.where(core == 0, ends[1], ends[0])]))
    *state, u2 = call(rim_kernel, [block] * 7, [block] * 3, scal, fine, via_a, via_b)
    *coefs, u2, pack = call(
        middle_kernel,
        [wide_mid] * 5 + [wide_low] * 4 + [block, (2, 8, 128)],
        [(5, 6, 64, 128)] + [wide_mid] * 5 + [wide_low] * 5 + [(20, MX, 128), (MROWS, 80, 128), block, block],
        scal, *state, u2, *parts,
    )
    parts = spread(pack)
    out, res = call(
        last_kernel,
        [(128, 128), (128, 128)],
        [(5, 2, 64, 128)] + [wide_mid] * 3 + [wide_low] * 3 + [(20, MX, 128), (MROWS, 80, 128), block, block],
        scal, *state, u2, *parts, *coefs,
    )
    return out.reshape(8, 16, 128), res.reshape(8, 16, 128)


def solution(mesh):
    spec = P("dev", "grp", None)
    return jax.shard_map(local, mesh=mesh, in_specs=(spec,) * 3, out_specs=(spec,) * 2, check_vma=False)
```
